256 devices in a mesh: dp: 32 (over z, x), mp: 8 (over y, core).
Axes of the slice: x: 4, y: 4, z: 8, core: 2. Of those that a mesh axis runs over, the one named last changes fastest.
Arguments:
- attn: bfloat16 [2, 4096, 4096], P(None, 'dp', 'mp'), may hold values from -6 to 6
- stream: bfloat16 [2, 4096, 4096], P(None, 'dp', 'mp'), may hold values from -13 to 13
- out_proj: bfloat16 [4096, 4096], P(None, 'mp'), may hold values from -0.09375 to 0.09375
- gain: float32 [4096], P('mp'), may hold values from 0.25 to 1.75
- neg_owner: int32 [4096, 8], P('dp'), may hold values from 0 to 31, as said below
- neg_row: int32 [4096, 8], P('dp'), may hold values from 0 to 127
Outputs:
- query_loss: float32 [4096], P('dp')
- grad_stream: float32 [2, 4096, 4096], P(None, 'dp', 'mp')
- grad_attn: float32 [2, 4096, 4096], P(None, 'dp', 'mp')
- grad_out_proj: float32 [4096, 4096], P('dp', 'mp')
The draws below stay inside these ranges and needn't reach their ends.
Inputs may be any that keep to these rules, and one draw needn't show every extreme that they name: `neg_owner`: the 8 hard negatives of a query have distinct owners; among the 128 queries of one index of dp, no owner is named more than 64 times.
All inputs are finite; a program needn't handle non-finite values.
Results may differ from the reference program's by a relative error of at most 0.018.
Values may be sent and summed in bfloat16 or wider, within the bound.
No kernel may reach another device: no remote copies, remote signals or barrier semaphores. Data moves between devices by JAX's collectives and lax.ppermute only.
A program may use at most 64 MiB of HBM per device.

```python
import jax
import jax.numpy as jnp
from jax import lax

D = 4096
K = 8
QUERIES_PER_PART = 128
TOKENS = 4096
CAP = 64
N_DP = 32


def hard_links(key):
    block_keys = jax.random.split(jax.random.fold_in(key, 101), N_DP)
    orders = jax.vmap(lambda block_key: jax.random.permutation(block_key, QUERIES_PER_PART))(block_keys)
    ranks = jnp.argsort(orders, axis=1).astype(jnp.int32)
    hot_owner = jax.random.randint(jax.random.fold_in(key, 102), (), 0, N_DP).astype(jnp.int32)
    offsets = jax.random.randint(jax.random.fold_in(key, 103), (N_DP, 1, 1), 0, N_DP - 1).astype(jnp.int32)
    turns = jax.random.randint(jax.random.fold_in(key, 104), (N_DP, QUERIES_PER_PART, 1), 0, K).astype(jnp.int32)
    is_hot = ranks < CAP
    start = jnp.where(is_hot, ranks * (K - 1), CAP * (K - 1) + (ranks - CAP) * K).astype(jnp.int32)
    column = jnp.arange(K, dtype=jnp.int32)[None, None, :]
    other_pos = start[:, :, None] + jnp.where(is_hot[:, :, None], column - 1, column)
    other_owner = (hot_owner + 1 + (offsets + other_pos) % (N_DP - 1)) % N_DP
    entries = jnp.where(is_hot[:, :, None] & (column == 0), hot_owner, other_owner).astype(jnp.int32)
    picked = ((column + turns) % K).astype(jnp.int32)
    owners = jnp.take_along_axis(entries, picked, axis=2).reshape(TOKENS, K).astype(jnp.int32)
    rows = jax.random.randint(jax.random.fold_in(key, 105), (TOKENS, K), 0, QUERIES_PER_PART).astype(jnp.int32)
    return (owners, rows)


def build_stream(passages, noise, mixing, own_share, passage_ids):
    queries = own_share * passages + noise
    for column in range(K):
        queries = queries + mixing[:, column:column + 1] * passages[passage_ids[:, column]]
    return jnp.stack([queries, passages]).astype(jnp.bfloat16)


def draw_stream(key, part):
    owners, rows = hard_links(key)
    key = jax.random.fold_in(key, 3)
    base_key, noise_key, mix_key = jax.random.split(key, 3)
    passage_ids = (owners * QUERIES_PER_PART + rows).astype(jnp.int32)
    passages = jax.random.truncated_normal(base_key, -4.0, 4.0, (TOKENS, D), jnp.float32)
    noise = jax.random.truncated_normal(noise_key, -4.0, 4.0, (TOKENS, D), jnp.float32)
    mixing = jax.random.uniform(mix_key, (TOKENS, K), jnp.float32, 0.1, 0.25)
    return build_stream(passages, noise, mixing, 0.25, passage_ids)


def draw_neg_owner(key, part):
    owners, rows = hard_links(key)
    return owners


def draw_neg_row(key, part):
    owners, rows = hard_links(key)
    return rows


def raised(drawn, rng, source, target, parts, factor):
    def block_of(dim):
        return (jnp.arange(drawn.shape[dim]) // (drawn.shape[dim] // parts)).reshape((-1,) + (1,) * (drawn.ndim - 1 - dim))

    one_side = jax.random.permutation(rng, parts)[block_of(target)]
    far = (block_of(target) + parts // 2) % parts
    return jnp.where((block_of(source) == one_side) | (block_of(source) == far), factor * drawn, drawn)


def shard_levels(key, dims, pieces, smallest, high):
    def one(dim, blocks):
        draws = jax.random.uniform(jax.random.fold_in(jax.random.fold_in(key, 6), dim), (blocks,), jnp.float32, smallest / len(pieces), high / len(pieces))
        return jnp.repeat(jnp.exp(draws), dims[dim] // blocks).reshape((-1,) + (1,) * (len(dims) - dim - 1))

    level = one(*pieces[0])
    for cut in pieces[1:]:
        level = level * one(*cut)
    return level


def bell_draw(stream_key, dims, deviation, bound, cuts=(), kind=jnp.bfloat16):
    factor_of = shard_levels(stream_key, dims, cuts, -0.22, 0.18) if cuts else 1.0
    array = jax.random.normal(stream_key, dims, jnp.float32) * deviation * factor_of
    return jnp.minimum(jnp.maximum(array, -bound), bound).astype(kind)


def bell_draw_with(own_key, shape, deviation, limit, cuts, heavy, kind=jnp.bfloat16):
    values = deviation * jax.random.normal(own_key, shape, jnp.float32)
    if cuts:
        values = values * shard_levels(own_key, shape, cuts, -0.22, 0.18)
    return jnp.clip(raised(values, jax.random.fold_in(own_key, 3), *heavy), -limit, limit).astype(kind)


def setup_inputs(seed: int = 0) -> dict:
    key_list = jax.random.split(jax.random.key(seed), 7)
    attn = bell_draw_with(key_list[0], (2, TOKENS, D), 1.0, 6.0, ((1, 32), (2, 8)), (1, 2, 32, 2.75))
    stream = draw_stream(jax.random.fold_in(key_list[6], 71), 0)
    out_proj = bell_draw(key_list[2], (D, D), D ** -0.5, 0.09375, ((1, 8),))
    gain = jnp.clip(1.0 + 0.15 * jax.random.normal(key_list[3], (D,), jnp.float32), 0.25, 1.75)
    neg_owner = draw_neg_owner(jax.random.fold_in(key_list[6], 71), 0)
    neg_row = draw_neg_row(jax.random.fold_in(key_list[6], 71), 0)
    return {"attn": attn, "stream": stream, "out_proj": out_proj, "gain": gain, "neg_owner": neg_owner, "neg_row": neg_row}


SOFTMAX_WARMTH = 0.02
OBJECTIVE_SCALE = 16.0
EPSILON = 1e-06

def rounded_features(values):
    return lax.optimization_barrier(values.astype(jnp.bfloat16)).astype(jnp.float32)

def reference(attn, stream, out_proj, gain, neg_owner, neg_row):
    kind_count, token_count, full_width = attn.shape
    flat_attn = attn.reshape(kind_count * token_count, full_width)
    hidden = jnp.dot(flat_attn, out_proj, preferred_element_type=jnp.float32) + stream.reshape(kind_count * token_count, full_width).astype(jnp.float32)
    scaled = hidden * gain[None, :]
    row_norm = jnp.sqrt(lax.optimization_barrier(jnp.sum(scaled * scaled, axis=1, keepdims=True)) + EPSILON)
    unit_rows = scaled / row_norm
    embedded = rounded_features(unit_rows)
    queries = embedded[:token_count]
    passages = embedded[token_count:]
    groups_count = token_count // QUERIES_PER_PART
    query_blocks = queries.reshape(groups_count, QUERIES_PER_PART, full_width)
    passage_blocks = passages.reshape(groups_count, QUERIES_PER_PART, full_width)
    in_group_scores = jnp.einsum('gqd,gpd->gqp', query_blocks, passage_blocks)
    passage_ids = (neg_owner * QUERIES_PER_PART + neg_row).astype(jnp.int32)
    hard_columns = []
    for column in range(K):
        picked_rows = passages[passage_ids[:, column]]
        hard_columns.append(lax.optimization_barrier(jnp.sum(queries * picked_rows, axis=1)))
    hard_negative_scores = jnp.stack(hard_columns, axis=1)
    in_group_logits = in_group_scores / SOFTMAX_WARMTH
    hard_negative_logits = hard_negative_scores / SOFTMAX_WARMTH
    sum_exp = lax.optimization_barrier(jnp.sum(jnp.exp(in_group_logits), axis=2)).reshape(token_count) + lax.optimization_barrier(jnp.sum(jnp.exp(hard_negative_logits), axis=1))
    log_partition_total = jnp.log(sum_exp)
    positive = jnp.diagonal(in_group_logits, axis1=1, axis2=2).reshape(token_count)
    query_loss = log_partition_total - positive
    identity_matrix = jnp.eye(QUERIES_PER_PART, dtype=jnp.float32)
    in_group_gradient = rounded_features(OBJECTIVE_SCALE * (jnp.exp(in_group_logits - log_partition_total.reshape(groups_count, QUERIES_PER_PART, 1)) - identity_matrix[None]) / SOFTMAX_WARMTH)
    hard_negative_gradient = rounded_features(OBJECTIVE_SCALE * jnp.exp(hard_negative_logits - log_partition_total[:, None]) / SOFTMAX_WARMTH)
    grad_queries = jnp.einsum('gqp,gpd->gqd', in_group_gradient, passage_blocks).reshape(token_count, full_width)
    grad_passages = jnp.einsum('gqp,gqd->gpd', in_group_gradient, query_blocks).reshape(token_count, full_width)
    for column in range(K):
        grad_queries = grad_queries + hard_negative_gradient[:, column:column + 1] * passages[passage_ids[:, column]]
        grad_passages = grad_passages + jax.ops.segment_sum(hard_negative_gradient[:, column:column + 1] * queries, passage_ids[:, column], num_segments=token_count)
    grad_embed = jnp.concatenate([grad_queries, grad_passages], axis=0)
    projection = lax.optimization_barrier(jnp.sum(grad_embed * unit_rows, axis=1, keepdims=True))
    grad_stream = gain[None, :] * (grad_embed - projection * unit_rows) / row_norm
    grad_rounded = grad_stream.astype(jnp.bfloat16)
    grad_attn = jnp.dot(grad_rounded, out_proj.T, preferred_element_type=jnp.float32)
    grad_out_proj = jnp.dot(flat_attn.T, grad_rounded, preferred_element_type=jnp.float32)
    return (query_loss, grad_stream.reshape(kind_count, token_count, full_width), grad_attn.reshape(kind_count, token_count, full_width), grad_out_proj)
```

```python
import jax
import jax.numpy as jnp
from jax import lax
from jax.experimental import pallas as pl
from jax.experimental.pallas import tpu as pltpu
from jax.sharding import Mesh
from jax.sharding import PartitionSpec as P

WARMTH = 0.02
GRAD_SCALE = 16.0 / WARMTH
EPSILON = 1e-06
F32 = jnp.float32
BF16 = jnp.bfloat16
DP = ("z", "x")
MP = ("y", "core")
NZ, NX, NY, NC = 8, 4, 4, 2
N_DP, N_MP = NZ * NX, NY * NC
ROWS = 128
NEG = 8
ALL_ROWS = N_DP * ROWS
FEATURES = 512
WIDTH = N_MP * FEATURES
TILE = 512


def shifted(size, step):
    return [(i, (i + step) % size) for i in range(size)]


def place(buffer, block, index):
    return lax.dynamic_update_slice(buffer, block[None], (index,) + (0,) * block.ndim)


def rows_first(block, index, size):
    left = lax.ppermute(block, "x", shifted(NX, 1))
    right = lax.ppermute(block, "x", shifted(NX, -1))
    half = block.shape[0] // 2
    far = jnp.concatenate(
        [
            lax.ppermute(left[:half], "x", shifted(NX, 1)),
            lax.ppermute(right[half:], "x", shifted(NX, -1)),
        ],
        axis=0,
    )
    buffer = jnp.zeros((NZ, NX) + block.shape[1:], block.dtype)
    for part, s in ((block, 0), (left, 1), (right, -1), (far, 2)):
        buffer = lax.dynamic_update_slice(buffer, part[:, None], (0, (index - s) % NX, 0, 0))
    return buffer


def gather_x(block):
    x = lax.axis_index("x")
    parts = [lax.ppermute(block, "x", shifted(NX, s)) for s in (1, 3, 2)]
    buffer = jnp.zeros((NX,) + block.shape, block.dtype)
    for s, part in zip((0, 1, 3, 2), [block] + parts):
        buffer = place(buffer, part, (x - s) % NX)
    return buffer


def gather_z(block):
    z = lax.axis_index("z")
    buffer = place(jnp.zeros((NZ,) + block.shape, block.dtype), block, z)
    up = down = block
    for s in range(1, NZ // 2 + 1):
        up = lax.ppermute(up, "z", shifted(NZ, 1))
        buffer = place(buffer, up, (z - s) % NZ)
        if s < NZ // 2:
            down = lax.ppermute(down, "z", shifted(NZ, -1))
            buffer = place(buffer, down, (z + s) % NZ)
    return buffer


def spread_dp(block):
    copies = jnp.broadcast_to(block[None], (N_DP,) + block.shape)
    return lax.all_to_all(copies, DP, 0, 0, tiled=True)


HALF = N_DP // 2


def coef_kernel(
    core_ref, owner_ref, row_ref, late_ref, exps_ref, aq_ref, apt_ref, ap_ref, invp_ref, tin_ref,
    left_ref, xp_ref, coef, xq, rows, hards,
):
    step = pl.program_id(0)
    groups = TILE // ROWS
    core = core_ref[0]

    @pl.when(step == 0)
    def _():
        xq[...] = jnp.zeros_like(xq)

    late = jnp.concatenate([late_ref[g] for g in range(groups)], axis=1)
    owner = jnp.concatenate([owner_ref[g] for g in range(groups)], axis=1)
    row = jnp.concatenate([row_ref[g] for g in range(groups)], axis=1)
    order = lax.broadcasted_iota(jnp.int32, (N_DP, TILE), 0)
    named = jnp.full((N_DP, TILE), -1, jnp.int32)
    hard = jnp.zeros((N_DP, TILE), F32)
    carried = jnp.zeros((N_DP, TILE), F32)
    for k in range(NEG):
        hit = owner[k : k + 1] == order
        named = jnp.where(hit, row[k : k + 1], named)
        hard = jnp.where(hit, late[k : k + 1], hard)
        carried = jnp.where(hit, late[NEG + k : NEG + k + 1], carried)
    rows[...] = named
    hards[...] = hard
    high = carried.astype(BF16)
    low = (carried - high.astype(F32)).astype(BF16)
    pad = jnp.zeros((ROWS - 2 * N_DP, TILE), F32)
    extra = jnp.concatenate([high.astype(F32), low.astype(F32), pad], axis=0).T.astype(BF16)
    aq_ext = jnp.concatenate([aq_ref[...], extra], axis=1)

    row_of = lax.broadcasted_iota(jnp.int32, (ROWS, TILE), 0)

    def build(o, _):
        at = pl.ds(core * HALF + o, 1)
        tile = jnp.where(row_of == rows[at, :], hards[at, :], 0.0).astype(BF16)
        coef[pl.ds(pl.multiple_of(o * ROWS, ROWS), ROWS), :] = tile
        return 0

    lax.fori_loop(0, HALF, build, 0, unroll=2)

    eye = lax.broadcasted_iota(jnp.int32, (ROWS, ROWS), 0) == lax.broadcasted_iota(
        jnp.int32, (ROWS, ROWS), 1
    )

    @pl.when(step // (HALF // groups) == core)
    def _():
        for part in range(groups):
            lanes = slice(part * ROWS, (part + 1) * ROWS)
            inner = jnp.where(
                eye, late[17:18, lanes], exps_ref[lanes, :].astype(F32) * late[16:17, lanes]
            )
            at = pl.ds(pl.multiple_of((step * groups + part - core * HALF) * ROWS, ROWS), ROWS)
            coef[at, lanes] = (coef[at, lanes].astype(F32) + inner).astype(BF16)

    def columns(c, _):
        at = pl.ds(pl.multiple_of(c * 512, 512), 512)
        xq[at, :] += jnp.dot(coef[at, :], aq_ext, preferred_element_type=F32)
        return 0

    lax.fori_loop(0, HALF * ROWS // 512, columns, 0)
    xp_ref[...] = jnp.dot(apt_ref[...], coef[...], preferred_element_type=F32).astype(BF16)

    @pl.when(step == pl.num_programs(0) - 1)
    def _():
        lane = lax.broadcasted_iota(jnp.int32, (ROWS, ROWS), 1)

        def finish(o, _):
            at = pl.ds(pl.multiple_of(o * ROWS, ROWS), ROWS)
            all_o = core * HALF + o
            sums = xq[at, ROWS:]
            mine = (lane == all_o) | (lane == N_DP + all_o)
            hard = jnp.sum(jnp.where(mine, sums, 0.0), axis=1, keepdims=True)
            across = lambda ref: jnp.sum(
                jnp.where(eye, ref[pl.ds(all_o, 1), :], 0.0), axis=1, keepdims=True
            )
            cp = hard * across(invp_ref) + across(tin_ref)
            left_ref[at, :] = (xq[at, :ROWS] - ap_ref[at, :].astype(F32) * cp).astype(BF16)
            return 0

        lax.fori_loop(0, HALF, finish, 0)


def coefficients(core, owner, row, late, exps, aq, apt, ap, invp, tin):
    full = lambda shape: pl.BlockSpec(shape, lambda t: (0, 0))
    group = lambda n: pl.BlockSpec((TILE // ROWS, n, ROWS), lambda t: (t, 0, 0))
    tall = lambda n: pl.BlockSpec((TILE, n), lambda t: (t, 0))
    held = HALF * ROWS
    return pl.pallas_call(
        coef_kernel,
        grid=(ALL_ROWS // TILE,),
        in_specs=[
            pl.BlockSpec(memory_space=pltpu.SMEM), group(NEG), group(NEG), group(24), tall(ROWS),
            tall(ROWS), full((ROWS, held)), full((held, ROWS)), full((N_DP, ROWS)),
            full((N_DP, ROWS)),
        ],
        out_specs=[full((held, ROWS)), pl.BlockSpec((ROWS, TILE), lambda t: (0, t))],
        out_shape=[
            jax.ShapeDtypeStruct((held, ROWS), BF16),
            jax.ShapeDtypeStruct((ROWS, ALL_ROWS), BF16),
        ],
        scratch_shapes=[
            pltpu.VMEM((held, TILE), BF16),
            pltpu.VMEM((held, 2 * ROWS), F32),
            pltpu.VMEM((N_DP, TILE), jnp.int32),
            pltpu.VMEM((N_DP, TILE), F32),
        ],
        compiler_params=pltpu.CompilerParams(vmem_limit_bytes=40 * 2**20),
        cost_estimate=pl.CostEstimate(
            flops=20 * 10**9, bytes_accessed=8 * 2**20, transcendentals=0
        ),
        name="coefficients",
    )(core.reshape(1), owner, row, late, exps, aq, apt, ap, invp, tin)


STEPS_Y = (0, 1, 3, 2)


def body(attn, stream, out_proj, gain, neg_owner, neg_row):
    z, x = lax.axis_index("z"), lax.axis_index("x")
    y, core = lax.axis_index("y"), lax.axis_index("core")
    d, m = z * NX + x, y * NC + core

    blocks = out_proj.reshape(NY, NC, FEATURES, FEATURES)

    def by_core(c):
        kept = [
            lax.dynamic_slice(blocks, ((y - s) % NY, c, 0, 0), (1, 1, FEATURES, FEATURES))
            for s in STEPS_Y
        ]
        return jnp.concatenate(kept, axis=0).reshape(NY * FEATURES, FEATURES)

    proj_mine, proj_other = by_core(core), by_core(1 - core)

    def project(block, res):
        parts = [block] + [lax.ppermute(block, "y", shifted(NY, s)) for s in STEPS_Y[1:]]
        near = jnp.concatenate(parts, axis=1)
        far = lax.ppermute(near, "core", shifted(NC, 1))
        hidden = jnp.dot(near, proj_mine, preferred_element_type=F32)
        hidden = hidden + jnp.dot(far, proj_other, preferred_element_type=F32)
        scaled = (hidden + res.astype(F32)) * gain[None, :]
        return (near, far), scaled, scaled.astype(BF16)

    pair_p, scaled_p, passages = project(attn[1], stream[1])
    attn_q, _ = lax.optimization_barrier((attn[0], pair_p[0]))
    pair_q, scaled_q, queries = project(attn_q, stream[0])

    column = gather_x(passages).reshape(NX * ROWS, FEATURES)
    p_all = lax.all_gather(column, "z", axis=0, tiled=True)
    q_all = rows_first(gather_z(queries), x, NX).reshape(ALL_ROWS, FEATURES)

    def some_rows(pair):
        cut = [lax.dynamic_slice_in_dim(v, m * 16, 16, 0).reshape(16, NY, FEATURES) for v in pair]
        both = [jnp.where(core == 0, cut[c], cut[1 - c]) for c in range(NC)]
        both = jnp.stack(both)
        at = lambda a: jnp.where((y - a) % NY == 3, 2, jnp.where((y - a) % NY == 2, 3, (y - a) % NY))
        rows = [lax.dynamic_index_in_dim(both, at(a), 2, keepdims=False) for a in range(NY)]
        return jnp.stack(rows)

    mine = jnp.stack([some_rows(pair_q), some_rows(pair_p)])
    mine = mine.reshape(2, NZ, 16, NX, ROWS).transpose(1, 3, 0, 2, 4).reshape(N_DP, 2, 16, ROWS)
    mine = lax.all_to_all(mine, DP, 0, 0, tiled=True)
    columns = lax.all_gather(mine, MP, axis=0)
    columns = columns.transpose(2, 1, 0, 3, 4).reshape(2, ALL_ROWS, ROWS)
    aq = columns[0]
    aqt = aq.T
    ap = lax.dynamic_slice_in_dim(columns[1], core * HALF * ROWS, HALF * ROWS, 0)
    apt = ap.T

    owner, row = neg_owner.T, neg_row.T
    order = jnp.arange(N_DP, dtype=jnp.int32)

    def dense(owners, values, empty):
        hit = owners[None] == order.reshape((N_DP,) + (1,) * owners.ndim)
        return jnp.sum(jnp.where(hit, values[None] - empty, 0), axis=1) + empty

    rows_own = dense(owner, row, -1)

    inner_part = lax.dot_general(
        passages, queries, (((1,), (1,)), ((), ())), preferred_element_type=F32
    )
    squares = jnp.stack([jnp.sum(scaled_q * scaled_q, axis=1), jnp.sum(scaled_p * scaled_p, axis=1)])
    part = jnp.concatenate([inner_part, squares, jnp.zeros((6, ROWS), F32)], axis=0)
    total = jnp.sum(lax.all_gather(part, MP, axis=0), axis=0)
    norm_q = jnp.sqrt(total[ROWS] + EPSILON)
    norm_p = jnp.sqrt(total[ROWS + 1] + EPSILON)
    inv_q, inv_p = 1.0 / norm_q, 1.0 / norm_p
    score = total[:ROWS] * inv_p[:, None] * inv_q[None, :]
    logit = score / WARMTH
    eye = jnp.eye(ROWS, dtype=bool)
    positive = jnp.sum(jnp.where(eye, logit, 0.0), axis=0)
    top = jnp.max(logit, axis=0)
    exps = jnp.exp(logit - top[None, :])
    exp_sum = jnp.sum(exps, axis=0)
    exps = (exps * inv_p[:, None] * inv_q[None, :]).astype(BF16)
    invp_all = spread_dp(inv_p)

    ids = (owner * ROWS + row)[m % NEG]
    share = jnp.concatenate(
        [
            lax.dynamic_slice_in_dim(exps, m * 16, 16, 0),
            jnp.stack([(ids // ROWS).astype(BF16), (ids % ROWS).astype(BF16)]),
            jnp.zeros((14, ROWS), BF16),
        ],
        axis=0,
    )
    shares = lax.all_gather(spread_dp(share), MP, axis=0)
    exps_all = shares[:, :, :16].transpose(1, 0, 2, 3).reshape(ALL_ROWS, ROWS)
    owner_all = shares[:, :, 16].transpose(1, 0, 2).astype(jnp.int32)
    row_all = shares[:, :, 17].transpose(1, 0, 2).astype(jnp.int32)

    row_iota = jnp.arange(ROWS, dtype=jnp.int32)
    named = rows_own[:, None, :] == row_iota[None, :, None]
    invp_named = jnp.sum(jnp.where(named, invp_all[:, :, None], 0.0), axis=1)
    raw = lax.dot_general(p_all, queries, (((1,), (1,)), ((), ())), preferred_element_type=F32)
    raw = jnp.sum(jnp.where(named, raw.reshape(N_DP, ROWS, ROWS), 0.0), axis=1)

    def pick(values):
        hit = owner[:, None, :] == order[None, :, None]
        return jnp.sum(jnp.where(hit, values[None], 0.0), axis=1)

    invp_hard = pick(invp_named)
    hard_score = lax.psum(pick(raw), MP) * invp_hard * inv_q[None]
    hard_logit = hard_score / WARMTH
    peak = jnp.maximum(top, jnp.max(hard_logit, axis=0))
    log_total = peak + jnp.log(
        exp_sum * jnp.exp(top - peak) + jnp.sum(jnp.exp(hard_logit - peak[None]), axis=0)
    )
    query_loss = log_total - positive
    hard = GRAD_SCALE * jnp.exp(hard_logit - log_total[None]) * inv_q[None] * invp_hard
    hard = hard.astype(BF16).astype(F32)
    factor = GRAD_SCALE * jnp.exp(top - log_total)
    diag = GRAD_SCALE * (jnp.exp(positive - log_total) - 1.0) * inv_q * inv_p
    inner = jnp.where(eye, diag[None], exps.astype(F32) * factor[None])
    inner_rounded = inner.astype(BF16).astype(F32)
    weighted = inner_rounded * score * norm_p[:, None]
    is_own = owner == d
    cq = (jnp.sum(weighted, axis=0) + jnp.sum(hard * hard_score / invp_hard, axis=0)) * inv_q
    own_row = jnp.sum(jnp.where(is_own, row + 1, 0), axis=0) - 1
    own_hard = jnp.sum(jnp.where(is_own, hard * hard_score, 0.0), axis=0)
    inner_p = inner_rounded * score + jnp.where(row_iota[:, None] == own_row[None], own_hard[None], 0.0)
    tin = jnp.sum(inner_p * norm_q[None], axis=1) * inv_p
    carried = jnp.where(is_own, 0.0, hard_score * norm_q[None])

    late = jnp.concatenate(
        [hard, carried, jnp.stack([factor, diag, cq, tin]), jnp.zeros((4, ROWS), F32)], axis=0
    )
    late_half = lax.dynamic_slice_in_dim(late, core * 12, 12, 0)
    late_half = spread_dp(late_half)
    late_other = lax.ppermute(late_half, "core", shifted(NC, 1))
    late_all = jnp.concatenate(
        [jnp.where(core == 0, late_half, late_other), jnp.where(core == 0, late_other, late_half)],
        axis=1,
    )

    coef_q = jnp.where(named, dense(owner, hard, 0.0)[:, None, :], 0.0)
    coef_q = coef_q + jnp.where((order == d)[:, None, None], inner[None], 0.0)
    coef_q = coef_q.astype(BF16).reshape(ALL_ROWS, ROWS)
    grad_q = lax.dot_general(coef_q, p_all, (((0,), (0,)), ((), ())), preferred_element_type=F32)
    to_me = owner_all == d
    row_me = (jnp.sum(jnp.where(to_me, row_all + 1, 0), axis=1) - 1).reshape(1, ALL_ROWS)
    hard_me = jnp.sum(jnp.where(to_me, late_all[:, :8], 0.0), axis=1).reshape(1, ALL_ROWS)
    sum_me = jnp.sum(jnp.where(to_me, late_all[:, :8] * late_all[:, 8:16], 0.0), axis=1)
    sum_me = sum_me.reshape(1, ALL_ROWS)
    named_me = row_me == row_iota[:, None]
    coef_p = jnp.where(named_me, hard_me, 0.0).reshape(ROWS, N_DP, ROWS)
    coef_p = coef_p + jnp.where((order == d)[None, :, None], inner[:, None, :], 0.0)
    coef_p = coef_p.astype(BF16).reshape(ROWS, ALL_ROWS)
    grad_p = jnp.dot(coef_p, q_all, preferred_element_type=F32)
    cp = tin + jnp.sum(jnp.where(named_me, sum_me, 0.0), axis=1) * inv_p
    grad_stream = jnp.concatenate(
        [
            gain[None] * (grad_q - cq[:, None] * scaled_q),
            gain[None] * (grad_p - cp[:, None] * scaled_p),
        ],
        axis=0,
    )
    rounded = grad_stream.astype(BF16)

    back = lambda w: lax.dot_general(
        rounded, w, (((1,), (1,)), ((), ())), preferred_element_type=F32
    )
    came = lax.ppermute(back(proj_other).astype(BF16), "core", shifted(NC, 1))
    kept = back(proj_mine) + came.astype(F32)
    grad_attn = kept[:, :FEATURES]
    for i, s in list(enumerate(STEPS_Y))[1:]:
        block = kept[:, i * FEATURES : (i + 1) * FEATURES].astype(BF16)
        grad_attn = grad_attn + lax.ppermute(block, "y", shifted(NY, -s)).astype(F32)

    left, right = coefficients(
        core, owner_all, row_all, late_all, exps_all, aq, apt, ap, invp_all, late_all[:, 19]
    )
    left_other = lax.ppermute(left, "core", shifted(NC, 1))
    right_other = lax.ppermute(right, "core", shifted(NC, 1))
    left = jnp.concatenate(
        [jnp.where(core == 0, left, left_other), jnp.where(core == 0, left_other, left)], axis=0
    )
    right = right.astype(F32) + right_other.astype(F32)
    right = right - aqt.astype(F32) * late_all[:, 18].reshape(1, ALL_ROWS)
    grad_weight = lax.dot_general(left, p_all, (((0,), (0,)), ((), ())), preferred_element_type=F32)
    grad_weight = grad_weight + jnp.dot(right.astype(BF16), q_all, preferred_element_type=F32)
    grad_weight = grad_weight * gain[None]
    return (
        query_loss,
        grad_stream.reshape(2, ROWS, FEATURES),
        grad_attn.reshape(2, ROWS, FEATURES),
        grad_weight,
    )


def solution(mesh):
    fine = Mesh(mesh.devices.reshape(NZ, NX, NY, NC), ("z", "x", "y", "core"))
    placed = (
        P(None, DP, MP),
        P(None, DP, MP),
        P(None, MP),
        P(MP),
        P(DP, None),
        P(DP, None),
    )
    return jax.shard_map(
        body,
        mesh=fine,
        in_specs=placed,
        out_specs=(P(DP), P(None, DP, MP), P(None, DP, MP), P(DP, MP)),
        check_vma=False,
    )
```

```python
import jax
import jax.numpy as jnp
from jax import lax
from jax.experimental import pallas as pl
from jax.experimental.pallas import tpu as pltpu
from jax.sharding import Mesh
from jax.sharding import PartitionSpec as P

WARMTH = 0.02
GRAD_SCALE = 16.0 / WARMTH
EPSILON = 1e-06
F32 = jnp.float32
BF16 = jnp.bfloat16
DP = ("z", "x")
MP = ("y", "core")
NZ, NX, NY, NC = 8, 4, 4, 2
N_DP, N_MP = NZ * NX, NY * NC
ROWS = 128
NEG = 8
ALL_ROWS = N_DP * ROWS
FEATURES = 512
WIDTH = N_MP * FEATURES
TILE = 1024
CHUNK = 4


def shifted(size, step):
    return [(i, (i + step) % size) for i in range(size)]


def place(buffer, block, index):
    return lax.dynamic_update_slice(buffer, block[None], (index,) + (0,) * block.ndim)


def gather_x(block):
    x = lax.axis_index("x")
    parts = [lax.ppermute(block, "x", shifted(NX, s)) for s in (1, 3, 2)]
    buffer = jnp.zeros((NX,) + block.shape, block.dtype)
    for s, part in zip((0, 1, 3, 2), [block] + parts):
        buffer = place(buffer, part, (x - s) % NX)
    return buffer


def pieces_x(line):
    left = lax.ppermute(line, "x", shifted(NX, 1))
    right = lax.ppermute(line, "x", shifted(NX, -1))
    low = lax.ppermute(left[: NZ // 2], "x", shifted(NX, 1))
    high = lax.ppermute(right[NZ // 2 :], "x", shifted(NX, -1))
    return line, left, right, low, high


PLACES_X = (0, 1, 3, 2)
DEEP = 2
LATE = 32


def late_rows(ref, j):
    r = ref[pl.ds(j, 1)].astype(F32)[0]
    return r[:8], r[8:16] + r[16:24], r[24:25] + r[25:26], r[26:27], r[27:28] + r[28:29], r[29:30] + r[30:31]


def index_rows(ref, j):
    r = ref[:, pl.ds(j, 1)].astype(F32)[:, 0]
    return r[:, 0].astype(jnp.int32), r[:, 1].astype(jnp.int32)


def shares_spec(groups, part, size=16):
    return pl.BlockSpec((N_MP, groups, size, ROWS), lambda t: (0, t, part, 0))


def piece_specs():
    block = (DEEP, ROWS, FEATURES)
    half = NZ // 2 // DEEP
    near = pl.BlockSpec(block, lambda t: (t, 0, 0))
    low = pl.BlockSpec(block, lambda t: (jnp.minimum(t, half - 1), 0, 0))
    high = pl.BlockSpec(block, lambda t: (jnp.maximum(t - half, 0), 0, 0))
    return [near, near, near, low, high]


def read_pieces(refs):
    line, left, right, low, high = refs
    is_low = pl.program_id(0) < NZ // 2 // DEEP
    rows = []
    for i in range(DEEP):
        rows += [line[i], left[i], right[i], jnp.where(is_low, low[i], high[i])]
    return jnp.concatenate(rows, axis=0)


def spread_dp(block):
    copies = jnp.broadcast_to(block[None], (N_DP,) + block.shape)
    return lax.all_to_all(copies, DP, 0, 0, tiled=True)


HALF = N_DP // 2


def coef_kernel(
    core_ref, index_ref, late_ref, exps_ref, aq_ref, ap_ref, invp_ref, whole_ref, left_ref, xp_ref,
    xq, apt_ref,
):
    step = pl.program_id(0)
    groups = TILE // ROWS
    core = core_ref[0]
    held = lambda o: ap_ref[:, pl.ds(core * HALF + o, 1)].reshape(ROWS, ROWS)

    @pl.when(step == 0)
    def _():
        xq[...] = jnp.zeros_like(xq)
        for o in range(HALF):
            apt_ref[:, o * ROWS : (o + 1) * ROWS] = held(o).astype(F32).T.astype(BF16)

    lates = [late_rows(late_ref, g) for g in range(groups)]
    indices = [index_rows(index_ref, g) for g in range(groups)]
    beside = lambda rows, i: jnp.concatenate([r[i] for r in rows], axis=1)
    hard_k, carried_k = beside(lates, 0), beside(lates, 1)
    owner, row = beside(indices, 0) - core * HALF, beside(indices, 1)
    aq = jnp.concatenate([aq_ref[:, g].reshape(ROWS, ROWS) for g in range(groups)], axis=0)
    order = lax.broadcasted_iota(jnp.int32, (HALF, TILE), 0)
    named = jnp.full((HALF, TILE), -1, jnp.int32)
    hard = jnp.zeros((HALF, TILE), F32)
    carried = jnp.zeros((HALF, TILE), F32)
    for k in range(NEG):
        hit = owner[k : k + 1] == order
        named = jnp.where(hit, row[k : k + 1], named)
        hard = jnp.where(hit, hard_k[k : k + 1], hard)
        carried = jnp.where(hit, carried_k[k : k + 1], carried)
    high = carried.astype(BF16)
    low = (carried - high.astype(F32)).astype(BF16)
    pad = jnp.zeros((ROWS - 2 * HALF, TILE), F32)
    extra = jnp.concatenate([high.astype(F32), low.astype(F32), pad], axis=0).T.astype(BF16)
    aq_ext = jnp.concatenate([aq, extra], axis=1)
    row_of = lax.broadcasted_iota(jnp.int32, (ROWS, TILE), 0)
    xp = jnp.zeros((ROWS, TILE), F32)
    for c in range(0, HALF, CHUNK):
        tiles = []
        for o in range(c, c + CHUNK):
            tile = jnp.where(row_of == named[o : o + 1], hard[o : o + 1], 0.0)
            tiles.append(tile.astype(BF16))
        coef = jnp.concatenate(tiles, axis=0)
        at = slice(c * ROWS, (c + CHUNK) * ROWS)
        xq[at, :] += jnp.dot(coef, aq_ext, preferred_element_type=F32)
        xp = xp + jnp.dot(apt_ref[:, at], coef, preferred_element_type=F32)
    xp_ref[...] = xp.astype(BF16)

    eye = lax.broadcasted_iota(jnp.int32, (ROWS, ROWS), 0) == lax.broadcasted_iota(
        jnp.int32, (ROWS, ROWS), 1
    )

    @pl.when(step // (HALF // groups) == core)
    def _():
        for part in range(groups):
            lanes = slice(part * ROWS, (part + 1) * ROWS)
            exps = exps_ref[:, part].reshape(ROWS, ROWS).astype(F32)
            inner = jnp.where(eye, lates[part][3], exps * lates[part][2]).astype(BF16)
            at = pl.ds(pl.multiple_of((step * groups + part - core * HALF) * ROWS, ROWS), ROWS)
            xq[at, :ROWS] += jnp.dot(inner, aq[lanes, :], preferred_element_type=F32)
            more = jnp.dot(apt_ref[:, at], inner, preferred_element_type=F32)
            more = more - aq[lanes, :].astype(F32).T * lates[part][4]
            xp_ref[:, lanes] = (xp_ref[:, lanes].astype(F32) + more).astype(BF16)

    @pl.when(step == pl.num_programs(0) - 1)
    def _():
        lane = lax.broadcasted_iota(jnp.int32, (ROWS, ROWS), 1)
        for o in range(HALF):
            at = slice(o * ROWS, (o + 1) * ROWS)
            sums = xq[at, ROWS:]
            mine = (lane == o) | (lane == HALF + o)
            hard_sum = jnp.sum(jnp.where(mine, sums, 0.0), axis=1, keepdims=True)
            across = lambda v: jnp.sum(jnp.where(eye, v, 0.0), axis=1, keepdims=True)
            all_o = core * HALF + o
            cp = hard_sum * across(invp_ref[pl.ds(all_o, 1), :]) + across(late_rows(whole_ref, all_o)[5])
            left_ref[at, :] = (xq[at, :ROWS] - held(o).astype(F32) * cp).astype(BF16)

def coefficients(core, shares, late, invp):
    full = lambda shape: pl.BlockSpec(shape, lambda t: (0,) * len(shape))
    held = HALF * ROWS
    groups = TILE // ROWS
    return pl.pallas_call(
        coef_kernel,
        grid=(ALL_ROWS // TILE,),
        in_specs=[
            pl.BlockSpec(memory_space=pltpu.SMEM), shares_spec(groups, 6, 8),
            pl.BlockSpec((groups, LATE, ROWS), lambda t: (t, 0, 0)),
            shares_spec(groups, 2), shares_spec(groups, 0),
            pl.BlockSpec((N_MP, N_DP, 16, ROWS), lambda t: (0, 0, 1, 0)), full((N_DP, ROWS)),
            full((N_DP, LATE, ROWS)),
        ],
        out_specs=[full((held, ROWS)), pl.BlockSpec((ROWS, TILE), lambda t: (0, t))],
        out_shape=[
            jax.ShapeDtypeStruct((held, ROWS), BF16),
            jax.ShapeDtypeStruct((ROWS, ALL_ROWS), BF16),
        ],
        scratch_shapes=[
            pltpu.VMEM((held, 2 * ROWS), F32),
            pltpu.VMEM((ROWS, held), BF16),
        ],
        compiler_params=pltpu.CompilerParams(vmem_limit_bytes=56 * 2**20),
        cost_estimate=pl.CostEstimate(
            flops=10 * 10**9, bytes_accessed=8 * 2**20, transcendentals=0
        ),
        name="coefficients",
    )(core.reshape(1), shares, late, shares, shares, shares, invp, late)

def own_kernel(
    d_ref, owner_ref, row_ref, hard_ref, inner_ref, index_ref, late_ref, sq_ref, sp_ref,
    gain_ref, cq_ref, tin_ref, invp_ref, q_ref, p0, p1, p2, p3, p4, stream_ref, rounded_ref,
    acc_q, acc_p, acc_t,
):
    step = pl.program_id(0)
    d, x = d_ref[0], d_ref[1]

    @pl.when(step == 0)
    def _():
        acc_q[...] = jnp.zeros_like(acc_q)
        acc_p[...] = jnp.zeros_like(acc_p)
        acc_t[...] = jnp.zeros_like(acc_t)

    row_of = lax.broadcasted_iota(jnp.int32, (ROWS, ROWS), 0)
    down = lambda v: jnp.sum(v, axis=0, keepdims=True)
    tall, wide = [], []
    for g in range(DEEP * NX):
        plane, n = step * DEEP + g // NX, g % NX
        block = plane * NX + (x + NX - PLACES_X[n]) % NX
        inner = jnp.where(block == d, inner_ref[...], 0.0)
        hit = owner_ref[...] == block
        named = down(jnp.where(hit, row_ref[...] + 1, 0)) - 1
        hard = down(jnp.where(hit, hard_ref[...], 0.0))
        tall.append((jnp.where(row_of == named, hard, 0.0) + inner).astype(BF16))
        inner = jnp.where(plane * NX + n == d, inner_ref[...], 0.0)
        owners, rows = index_rows(index_ref, g)
        hard_k, carried_k = late_rows(late_ref, g)[:2]
        hit = owners == d
        named = row_of == down(jnp.where(hit, rows + 1, 0)) - 1
        hard = down(jnp.where(hit, hard_k, 0.0))
        moved = down(jnp.where(hit, hard_k * carried_k, 0.0))
        wide.append((jnp.where(named, hard, 0.0) + inner).astype(BF16))
        acc_t[...] += jnp.where(named, moved, 0.0)
    acc_q[...] += lax.dot_general(
        jnp.concatenate(tall, axis=0), read_pieces((p0, p1, p2, p3, p4)), (((0,), (0,)), ((), ())),
        preferred_element_type=F32,
    )
    acc_p[...] += jnp.dot(jnp.concatenate(wide, axis=1), q_ref[...], preferred_element_type=F32)

    @pl.when(step == pl.num_programs(0) - 1)
    def _():
        eye = row_of == lax.broadcasted_iota(jnp.int32, (ROWS, ROWS), 1)
        across = lambda ref: jnp.sum(jnp.where(eye, ref[...], 0.0), axis=1, keepdims=True)
        cp = across(tin_ref) + jnp.sum(acc_t[...], axis=1, keepdims=True) * across(invp_ref)
        grad_q = gain_ref[...] * (acc_q[...] - across(cq_ref) * sq_ref[...])
        grad_p = gain_ref[...] * (acc_p[...] - cp * sp_ref[...])
        stream_ref[:ROWS, :] = grad_q
        stream_ref[ROWS:, :] = grad_p
        rounded_ref[:ROWS, :] = grad_q.astype(BF16)
        rounded_ref[ROWS:, :] = grad_p.astype(BF16)


def own_gradients(at, owner, row, hard, inner, shares, late, sq, sp, gain, cq, tin, invp, q, p):
    full = lambda a: pl.BlockSpec(a.shape, lambda t: (0,) * a.ndim)
    size = DEEP * NX
    tall = pl.BlockSpec((size * ROWS, FEATURES), lambda t: (t, 0))
    whole = pl.BlockSpec((2 * ROWS, FEATURES), lambda t: (0, 0))
    return pl.pallas_call(
        own_kernel,
        grid=(NZ // DEEP,),
        in_specs=[pl.BlockSpec(memory_space=pltpu.SMEM)]
        + [full(a) for a in (owner, row, hard, inner)]
        + [shares_spec(size, 6, 8), pl.BlockSpec((size, LATE, ROWS), lambda t: (t, 0, 0))]
        + [full(a) for a in (sq, sp, gain, cq, tin, invp)]
        + [tall]
        + piece_specs(),
        out_specs=[whole, whole],
        out_shape=[
            jax.ShapeDtypeStruct((2 * ROWS, FEATURES), F32),
            jax.ShapeDtypeStruct((2 * ROWS, FEATURES), BF16),
        ],
        scratch_shapes=[
            pltpu.VMEM((ROWS, FEATURES), F32),
            pltpu.VMEM((ROWS, FEATURES), F32),
            pltpu.VMEM((ROWS, ROWS), F32),
        ],
        compiler_params=pltpu.CompilerParams(vmem_limit_bytes=56 * 2**20),
        cost_estimate=pl.CostEstimate(
            flops=2 * 10**9, bytes_accessed=10 * 2**20, transcendentals=0
        ),
        name="own_gradients",
    )(at, owner, row, hard, inner, shares, late, sq, sp, gain, cq, tin, invp, q, *p)


def final_kernel(
    x_ref, left_ref, near_ref, far_ref, gain_ref, q_ref, p0, p1, p2, p3, p4, out_ref
):
    step = pl.program_id(0)
    x = x_ref[0]

    @pl.when(step == 0)
    def _():
        out_ref[...] = jnp.zeros_like(out_ref)

    starts = [
        pl.multiple_of((i * NX + (x + NX - s) % NX) * ROWS, ROWS) for i in range(DEEP) for s in PLACES_X
    ]
    left = jnp.concatenate([left_ref[pl.ds(start, ROWS), :] for start in starts], axis=0)
    right = (near_ref[...].astype(F32) + far_ref[...].astype(F32)).astype(BF16)
    out_ref[...] += gain_ref[...] * (
        lax.dot_general(
            left, read_pieces((p0, p1, p2, p3, p4)), (((0,), (0,)), ((), ())),
            preferred_element_type=F32,
        )
        + jnp.dot(right, q_ref[...], preferred_element_type=F32)
    )


def final_product(at, left, near, far, gain, q, p):
    size = DEEP * NX * ROWS
    lanes = lambda n: pl.BlockSpec((n, size), lambda t: (0, t))
    tall = lambda n: pl.BlockSpec((size, n), lambda t: (t, 0))
    return pl.pallas_call(
        final_kernel,
        grid=(NZ // DEEP,),
        in_specs=[
            pl.BlockSpec(memory_space=pltpu.SMEM), tall(ROWS), lanes(ROWS), lanes(ROWS),
            pl.BlockSpec((1, FEATURES), lambda t: (0, 0)), tall(FEATURES),
        ]
        + piece_specs(),
        out_specs=pl.BlockSpec((ROWS, FEATURES), lambda t: (0, 0)),
        out_shape=jax.ShapeDtypeStruct((ROWS, FEATURES), F32),
        compiler_params=pltpu.CompilerParams(vmem_limit_bytes=56 * 2**20),
        cost_estimate=pl.CostEstimate(
            flops=2 * 10**9, bytes_accessed=12 * 2**20, transcendentals=0
        ),
        name="final_product",
    )(at, left, near, far, gain, q, *p)


STEPS_Y = (0, 1, 3, 2)


def body(attn, stream, out_proj, gain, neg_owner, neg_row):
    z, x = lax.axis_index("z"), lax.axis_index("x")
    y, core = lax.axis_index("y"), lax.axis_index("core")
    d, m = z * NX + x, y * NC + core

    blocks = out_proj.reshape(NY, NC, FEATURES, FEATURES)

    def by_core(c):
        kept = [
            lax.dynamic_slice(blocks, ((y - s) % NY, c, 0, 0), (1, 1, FEATURES, FEATURES))
            for s in STEPS_Y
        ]
        return jnp.concatenate(kept, axis=0).reshape(NY * FEATURES, FEATURES)

    proj_mine, proj_other = by_core(core), by_core(1 - core)

    def project(block, kind):
        parts = [block] + [lax.ppermute(block, "y", shifted(NY, s)) for s in STEPS_Y[1:]]
        near = jnp.concatenate(parts, axis=1)
        far = lax.ppermute(near, "core", shifted(NC, 1))
        hidden = jnp.dot(near, proj_mine, preferred_element_type=F32)
        hidden = hidden + jnp.dot(far, proj_other, preferred_element_type=F32)
        scaled = (hidden + stream[kind].astype(F32)) * gain[None, :]
        return (near, far), scaled, scaled.astype(BF16)

    pair_p, scaled_p, passages = project(attn[1], 1)
    p_line = lax.all_gather(passages, "z", axis=0)
    p_pieces = pieces_x(p_line)

    attn_q, _ = lax.optimization_barrier((attn[0], passages))
    pair_q, scaled_q, queries = project(attn_q, 0)
    column = gather_x(queries).reshape(NX * ROWS, FEATURES)
    q_all = lax.all_gather(column, "z", axis=0, tiled=True)

    def some_rows(pair):
        cut = [lax.dynamic_slice_in_dim(v, m * 16, 16, 0).reshape(16, NY, FEATURES) for v in pair]
        both = jnp.stack([jnp.where(core == 0, cut[c], cut[1 - c]) for c in range(NC)])
        at = lambda a: jnp.where((y - a) % NY == 3, 2, jnp.where((y - a) % NY == 2, 3, (y - a) % NY))
        rows = [lax.dynamic_index_in_dim(both, at(a), 2, keepdims=False) for a in range(NY)]
        return jnp.stack(rows)

    mine = jnp.stack([some_rows(pair_q), some_rows(pair_p)])
    mine = mine.reshape(2, NZ, 16, NX, ROWS).transpose(1, 3, 0, 2, 4).reshape(N_DP, 32, ROWS)

    owner, row = neg_owner.T, neg_row.T
    order = jnp.arange(N_DP, dtype=jnp.int32)

    def dense(owners, values, empty):
        hit = owners[None] == order.reshape((N_DP,) + (1,) * owners.ndim)
        return jnp.sum(jnp.where(hit, values[None] - empty, 0), axis=1) + empty

    rows_own = dense(owner, row, -1)

    inner_part = lax.dot_general(
        passages, queries, (((1,), (1,)), ((), ())), preferred_element_type=F32
    )
    squares = jnp.stack([jnp.sum(scaled_q * scaled_q, axis=1), jnp.sum(scaled_p * scaled_p, axis=1)])
    part = jnp.concatenate([inner_part, squares, jnp.zeros((6, ROWS), F32)], axis=0)
    part, _ = lax.optimization_barrier((part, column))
    total = jnp.sum(lax.all_gather(part, MP, axis=0), axis=0)
    norm_q = jnp.sqrt(total[ROWS] + EPSILON)
    norm_p = jnp.sqrt(total[ROWS + 1] + EPSILON)
    inv_q, inv_p = 1.0 / norm_q, 1.0 / norm_p
    score = total[:ROWS] * inv_p[:, None] * inv_q[None, :]
    logit = score / WARMTH
    eye = jnp.eye(ROWS, dtype=bool)
    positive = jnp.sum(jnp.where(eye, logit, 0.0), axis=0)
    top = jnp.max(logit, axis=0)
    exps = jnp.exp(logit - top[None, :])
    exp_sum = jnp.sum(exps, axis=0)
    exps = (exps * inv_p[:, None] * inv_q[None, :]).astype(BF16)

    ids = (owner * ROWS + row)[m % NEG]
    high = lax.reduce_precision(inv_p, 8, 7)
    middle = lax.reduce_precision(inv_p - high, 8, 7)
    small = [(ids // ROWS), (ids % ROWS), high, middle, inv_p - high - middle]
    share = jnp.concatenate(
        [
            lax.dynamic_slice_in_dim(exps, m * 16, 16, 0),
            jnp.stack([v.astype(BF16) for v in small]),
            jnp.zeros((3, ROWS), BF16),
        ],
        axis=0,
    )
    share = jnp.concatenate([mine, jnp.broadcast_to(share[None], (N_DP, 24, ROWS))], axis=1)
    share, _ = lax.optimization_barrier((share, p_line))
    share = lax.all_to_all(share, DP, 0, 0, tiled=True)
    invp_all = jnp.sum(share[:, 50:53].astype(F32), axis=1)
    shares = lax.all_gather(share, MP, axis=0)

    row_iota = jnp.arange(ROWS, dtype=jnp.int32)
    named = rows_own[:, None, :] == row_iota[None, :, None]
    invp_named = jnp.sum(jnp.where(named, invp_all[:, :, None], 0.0), axis=1)
    raw_hard = jnp.zeros((NEG, ROWS), F32)
    for piece, s, first in zip(p_pieces, (0, 1, 3, 2, 2), (0, 0, 0, 0, NZ // 2)):
        here = (first + jnp.arange(piece.shape[0])) * NX + (x - s) % NX
        hit = owner[None] == here[:, None, None]
        row_here = jnp.sum(jnp.where(hit, row[None] + 1, 0), axis=1) - 1
        raw = lax.dot_general(
            piece.reshape(-1, FEATURES), queries, (((1,), (1,)), ((), ())), preferred_element_type=F32
        ).reshape(-1, ROWS, ROWS)
        raw = jnp.sum(jnp.where(row_here[:, None] == row_iota[None, :, None], raw, 0.0), axis=1)
        raw_hard = raw_hard + jnp.sum(jnp.where(hit, raw[:, None], 0.0), axis=0)

    def pick(values):
        hit = owner[:, None, :] == order[None, :, None]
        return jnp.sum(jnp.where(hit, values[None], 0.0), axis=1)

    invp_hard = pick(invp_named)
    copies = jnp.broadcast_to(raw_hard[None], (N_MP, NEG, ROWS))
    raw = jnp.sum(lax.all_to_all(copies, MP, 0, 0, tiled=True), axis=0)
    hard_score = raw * invp_hard * inv_q[None]
    hard_logit = hard_score / WARMTH
    peak = jnp.maximum(top, jnp.max(hard_logit, axis=0))
    log_total = peak + jnp.log(
        exp_sum * jnp.exp(top - peak) + jnp.sum(jnp.exp(hard_logit - peak[None]), axis=0)
    )
    query_loss = log_total - positive
    hard = GRAD_SCALE * jnp.exp(hard_logit - log_total[None]) * inv_q[None] * invp_hard
    hard = hard.astype(BF16).astype(F32)
    factor = GRAD_SCALE * jnp.exp(top - log_total)
    diag = GRAD_SCALE * (jnp.exp(positive - log_total) - 1.0) * inv_q * inv_p
    inner = jnp.where(eye, diag[None], exps.astype(F32) * factor[None])
    inner_rounded = inner.astype(BF16).astype(F32)
    weighted = inner_rounded * score * norm_p[:, None]
    is_own = owner == d
    cq = (jnp.sum(weighted, axis=0) + jnp.sum(hard * hard_score / invp_hard, axis=0)) * inv_q
    own_row = jnp.sum(jnp.where(is_own, row + 1, 0), axis=0) - 1
    own_hard = jnp.sum(jnp.where(is_own, hard * hard_score, 0.0), axis=0)
    inner_p = inner_rounded * score + jnp.where(row_iota[:, None] == own_row[None], own_hard[None], 0.0)
    tin = jnp.sum(inner_p * norm_q[None], axis=1) * inv_p
    carried = jnp.where(is_own, 0.0, hard_score * norm_q[None])

    def pieces(v):
        high = lax.reduce_precision(v, 8, 7)
        return [high, v - high]

    late = [hard] + pieces(carried) + [jnp.stack(pieces(factor) + [diag] + pieces(cq) + pieces(tin) + [diag])]
    late = jnp.concatenate([v.astype(BF16) for v in late], axis=0)
    late_half = lax.dynamic_slice_in_dim(late, core * (LATE // 2), LATE // 2, 0)
    late_half = spread_dp(late_half)
    late_other = lax.ppermute(late_half, "core", shifted(NC, 1))
    late_all = jnp.concatenate(
        [jnp.where(core == 0, late_half, late_other), jnp.where(core == 0, late_other, late_half)],
        axis=1,
    )

    line = lambda v: v.reshape(1, -1)
    grad_stream, rounded = own_gradients(
        jnp.stack([d, x]), owner, row, hard, inner, shares, late_all, scaled_q, scaled_p,
        line(gain), line(cq), line(tin), line(inv_p), q_all, p_pieces,
    )

    back = lambda w: lax.dot_general(
        rounded, w, (((1,), (1,)), ((), ())), preferred_element_type=F32
    )
    came = lax.ppermute(back(proj_other).astype(BF16), "core", shifted(NC, 1))
    kept = back(proj_mine) + came.astype(F32)
    grad_attn = kept[:, :FEATURES]
    for i, s in list(enumerate(STEPS_Y))[1:]:
        block = kept[:, i * FEATURES : (i + 1) * FEATURES].astype(BF16)
        grad_attn = grad_attn + lax.ppermute(block, "y", shifted(NY, -s)).astype(F32)

    late_used, _ = lax.optimization_barrier((late_all, kept))
    left, right = coefficients(core, shares, late_used, invp_all)
    left_other = lax.ppermute(left, "core", shifted(NC, 1))
    right_other = lax.ppermute(right, "core", shifted(NC, 1))
    left = jnp.concatenate(
        [jnp.where(core == 0, left, left_other), jnp.where(core == 0, left_other, left)], axis=0
    )
    grad_weight = final_product(
        x.reshape(1), left, right, right_other, line(gain), q_all, p_pieces
    )
    return (
        query_loss,
        grad_stream.reshape(2, ROWS, FEATURES),
        grad_attn.reshape(2, ROWS, FEATURES),
        grad_weight,
    )


def solution(mesh):
    fine = Mesh(mesh.devices.reshape(NZ, NX, NY, NC), ("z", "x", "y", "core"))
    placed = (
        P(None, DP, MP),
        P(None, DP, MP),
        P(None, MP),
        P(MP),
        P(DP, None),
        P(DP, None),
    )
    return jax.shard_map(
        body,
        mesh=fine,
        in_specs=placed,
        out_specs=(P(DP), P(None, DP, MP), P(None, DP, MP), P(DP, MP)),
        check_vma=False,
    )
```

```python
import jax
import jax.numpy as jnp
from jax import lax
from jax.experimental import pallas as pl
from jax.experimental.pallas import tpu as pltpu
from jax.sharding import Mesh
from jax.sharding import PartitionSpec as P

WARMTH = 0.02
GRAD_SCALE = 16.0 / WARMTH
EPSILON = 1e-06
F32 = jnp.float32
BF16 = jnp.bfloat16
DP = ("z", "x")
MP = ("y", "core")
NZ, NX, NY, NC = 8, 4, 4, 2
N_DP, N_MP = NZ * NX, NY * NC
ROWS = 128
NEG = 8
ALL_ROWS = N_DP * ROWS
FEATURES = 512
WIDTH = N_MP * FEATURES
TILE = 1024
CHUNK = 4


def shifted(size, step):
    return [(i, (i + step) % size) for i in range(size)]


def place(buffer, block, index):
    return lax.dynamic_update_slice(buffer, block[None], (index,) + (0,) * block.ndim)


def gather_x(block):
    x = lax.axis_index("x")
    parts = [lax.ppermute(block, "x", shifted(NX, s)) for s in (1, 3, 2)]
    buffer = jnp.zeros((NX,) + block.shape, block.dtype)
    for s, part in zip((0, 1, 3, 2), [block] + parts):
        buffer = place(buffer, part, (x - s) % NX)
    return buffer


def pieces_x(line):
    left = lax.ppermute(line, "x", shifted(NX, 1))
    right = lax.ppermute(line, "x", shifted(NX, -1))
    low = lax.ppermute(left[: NZ // 2], "x", shifted(NX, 1))
    high = lax.ppermute(right[NZ // 2 :], "x", shifted(NX, -1))
    return line, left, right, low, high


PLACES_X = (0, 1, 3, 2)
DEEP = 2
LATE = 32


def late_rows(ref, j):
    r = ref[pl.ds(j, 1)].astype(F32)[0]
    return r[:8], r[8:16] + r[16:24], r[24:25] + r[25:26], r[26:27], r[27:28] + r[28:29], r[29:30] + r[30:31]


def index_rows(ref, j):
    r = ref[:, pl.ds(j, 1)].astype(F32)[:, 0]
    return r[:, 0].astype(jnp.int32), r[:, 1].astype(jnp.int32)


def shares_spec(groups, part, size=16):
    return pl.BlockSpec((N_MP, groups, size, ROWS), lambda t: (0, t, part, 0))


def piece_specs():
    block = (DEEP, ROWS, FEATURES)
    half = NZ // 2 // DEEP
    near = pl.BlockSpec(block, lambda t: (t, 0, 0))
    low = pl.BlockSpec(block, lambda t: (jnp.minimum(t, half - 1), 0, 0))
    high = pl.BlockSpec(block, lambda t: (jnp.maximum(t - half, 0), 0, 0))
    return [near, near, near, low, high]


def read_pieces(refs):
    line, left, right, low, high = refs
    is_low = pl.program_id(0) < NZ // 2 // DEEP
    rows = []
    for i in range(DEEP):
        rows += [line[i], left[i], right[i], jnp.where(is_low, low[i], high[i])]
    return jnp.concatenate(rows, axis=0)


def spread_dp(block):
    copies = jnp.broadcast_to(block[None], (N_DP,) + block.shape)
    return lax.all_to_all(copies, DP, 0, 0, tiled=True)


HALF = N_DP // 2


def coef_kernel(
    core_ref, index_ref, late_ref, exps_ref, aq_ref, ap_ref, invp_ref, whole_ref, left_ref, xp_ref,
    xq, apt_ref,
):
    step = pl.program_id(0)
    groups = TILE // ROWS
    core = core_ref[0]
    held = lambda o: ap_ref[:, pl.ds(core * HALF + o, 1)].reshape(ROWS, ROWS)

    @pl.when(step == 0)
    def _():
        xq[...] = jnp.zeros_like(xq)
        for o in range(HALF):
            apt_ref[:, o * ROWS : (o + 1) * ROWS] = held(o).astype(F32).T.astype(BF16)

    lates = [late_rows(late_ref, g) for g in range(groups)]
    indices = [index_rows(index_ref, g) for g in range(groups)]
    beside = lambda rows, i: jnp.concatenate([r[i] for r in rows], axis=1)
    hard_k, carried_k = beside(lates, 0), beside(lates, 1)
    owner, row = beside(indices, 0) - core * HALF, beside(indices, 1)
    aq = jnp.concatenate([aq_ref[:, g].reshape(ROWS, ROWS) for g in range(groups)], axis=0)
    order = lax.broadcasted_iota(jnp.int32, (HALF, TILE), 0)
    named = jnp.full((HALF, TILE), -1, jnp.int32)
    hard = jnp.zeros((HALF, TILE), F32)
    carried = jnp.zeros((HALF, TILE), F32)
    for k in range(NEG):
        hit = owner[k : k + 1] == order
        named = jnp.where(hit, row[k : k + 1], named)
        hard = jnp.where(hit, hard_k[k : k + 1], hard)
        carried = jnp.where(hit, carried_k[k : k + 1], carried)
    high = carried.astype(BF16)
    low = (carried - high.astype(F32)).astype(BF16)
    pad = jnp.zeros((ROWS - 2 * HALF, TILE), F32)
    extra = jnp.concatenate([high.astype(F32), low.astype(F32), pad], axis=0).T.astype(BF16)
    aq_ext = jnp.concatenate([aq, extra], axis=1)
    row_of = lax.broadcasted_iota(jnp.int32, (ROWS, TILE), 0)
    xp = jnp.zeros((ROWS, TILE), F32)
    for c in range(0, HALF, CHUNK):
        tiles = []
        for o in range(c, c + CHUNK):
            tile = jnp.where(row_of == named[o : o + 1], hard[o : o + 1], 0.0)
            tiles.append(tile.astype(BF16))
        coef = jnp.concatenate(tiles, axis=0)
        at = slice(c * ROWS, (c + CHUNK) * ROWS)
        xq[at, :] += jnp.dot(coef, aq_ext, preferred_element_type=F32)
        xp = xp + jnp.dot(apt_ref[:, at], coef, preferred_element_type=F32)
    xp_ref[...] = xp.astype(BF16)

    eye = lax.broadcasted_iota(jnp.int32, (ROWS, ROWS), 0) == lax.broadcasted_iota(
        jnp.int32, (ROWS, ROWS), 1
    )

    @pl.when(step // (HALF // groups) == core)
    def _():
        for part in range(groups):
            lanes = slice(part * ROWS, (part + 1) * ROWS)
            exps = exps_ref[:, part].reshape(ROWS, ROWS).astype(F32)
            inner = jnp.where(eye, lates[part][3], exps * lates[part][2]).astype(BF16)
            at = pl.ds(pl.multiple_of((step * groups + part - core * HALF) * ROWS, ROWS), ROWS)
            xq[at, :ROWS] += jnp.dot(inner, aq[lanes, :], preferred_element_type=F32)
            more = jnp.dot(apt_ref[:, at], inner, preferred_element_type=F32)
            more = more - aq[lanes, :].astype(F32).T * lates[part][4]
            xp_ref[:, lanes] = (xp_ref[:, lanes].astype(F32) + more).astype(BF16)

    @pl.when(step == pl.num_programs(0) - 1)
    def _():
        lane = lax.broadcasted_iota(jnp.int32, (ROWS, ROWS), 1)
        for o in range(HALF):
            at = slice(o * ROWS, (o + 1) * ROWS)
            sums = xq[at, ROWS:]
            mine = (lane == o) | (lane == HALF + o)
            hard_sum = jnp.sum(jnp.where(mine, sums, 0.0), axis=1, keepdims=True)
            across = lambda v: jnp.sum(jnp.where(eye, v, 0.0), axis=1, keepdims=True)
            all_o = core * HALF + o
            cp = hard_sum * across(invp_ref[pl.ds(all_o, 1), :]) + across(late_rows(whole_ref, all_o)[5])
            left_ref[at, :] = (xq[at, :ROWS] - held(o).astype(F32) * cp).astype(BF16)

def coefficients(core, shares, late, invp):
    full = lambda shape: pl.BlockSpec(shape, lambda t: (0,) * len(shape))
    held = HALF * ROWS
    groups = TILE // ROWS
    return pl.pallas_call(
        coef_kernel,
        grid=(ALL_ROWS // TILE,),
        in_specs=[
            pl.BlockSpec(memory_space=pltpu.SMEM), shares_spec(groups, 6, 8),
            pl.BlockSpec((groups, LATE, ROWS), lambda t: (t, 0, 0)),
            shares_spec(groups, 2), shares_spec(groups, 0),
            pl.BlockSpec((N_MP, N_DP, 16, ROWS), lambda t: (0, 0, 1, 0)), full((N_DP, ROWS)),
            full((N_DP, LATE, ROWS)),
        ],
        out_specs=[full((held, ROWS)), pl.BlockSpec((ROWS, TILE), lambda t: (0, t))],
        out_shape=[
            jax.ShapeDtypeStruct((held, ROWS), BF16),
            jax.ShapeDtypeStruct((ROWS, ALL_ROWS), BF16),
        ],
        scratch_shapes=[
            pltpu.VMEM((held, 2 * ROWS), F32),
            pltpu.VMEM((ROWS, held), BF16),
        ],
        compiler_params=pltpu.CompilerParams(vmem_limit_bytes=56 * 2**20),
        cost_estimate=pl.CostEstimate(
            flops=10 * 10**9, bytes_accessed=8 * 2**20, transcendentals=0
        ),
        name="coefficients",
    )(core.reshape(1), shares, late, shares, shares, shares, invp, late)

def own_kernel(
    d_ref, owner_ref, row_ref, hard_ref, inner_ref, came_ref, sq_ref, sp_ref,
    gain_ref, cq_ref, tin_ref, invp_ref, q_ref, p0, p1, p2, p3, p4, stream_ref, rounded_ref,
    acc_q, acc_p, acc_t,
):
    step = pl.program_id(0)
    d, x = d_ref[0], d_ref[1]

    @pl.when(step == 0)
    def _():
        acc_q[...] = jnp.zeros_like(acc_q)
        acc_p[...] = jnp.zeros_like(acc_p)
        acc_t[...] = jnp.zeros_like(acc_t)

    row_of = lax.broadcasted_iota(jnp.int32, (ROWS, ROWS), 0)
    down = lambda v: jnp.sum(v, axis=0, keepdims=True)
    tall, wide = [], []
    for g in range(DEEP * NX):
        plane, n = step * DEEP + g // NX, g % NX
        block = plane * NX + (x + NX - PLACES_X[n]) % NX
        inner = jnp.where(block == d, inner_ref[...], 0.0)
        hit = owner_ref[...] == block
        named = down(jnp.where(hit, row_ref[...] + 1, 0)) - 1
        hard = down(jnp.where(hit, hard_ref[...], 0.0))
        tall.append((jnp.where(row_of == named, hard, 0.0) + inner).astype(BF16))
        inner = jnp.where(plane * NX + n == d, inner_ref[...], 0.0)
        came = came_ref[g].astype(F32)
        named = row_of == came[0:1].astype(jnp.int32)
        hard, moved = came[1:2], came[2:3] + came[3:4]
        wide.append((jnp.where(named, hard, 0.0) + inner).astype(BF16))
        acc_t[...] += jnp.where(named, moved, 0.0)
    acc_q[...] += lax.dot_general(
        jnp.concatenate(tall, axis=0), read_pieces((p0, p1, p2, p3, p4)), (((0,), (0,)), ((), ())),
        preferred_element_type=F32,
    )
    acc_p[...] += jnp.dot(jnp.concatenate(wide, axis=1), q_ref[...], preferred_element_type=F32)

    @pl.when(step == pl.num_programs(0) - 1)
    def _():
        eye = row_of == lax.broadcasted_iota(jnp.int32, (ROWS, ROWS), 1)
        across = lambda ref: jnp.sum(jnp.where(eye, ref[...], 0.0), axis=1, keepdims=True)
        cp = across(tin_ref) + jnp.sum(acc_t[...], axis=1, keepdims=True) * across(invp_ref)
        grad_q = gain_ref[...] * (acc_q[...] - across(cq_ref) * sq_ref[...])
        grad_p = gain_ref[...] * (acc_p[...] - cp * sp_ref[...])
        stream_ref[:ROWS, :] = grad_q
        stream_ref[ROWS:, :] = grad_p
        rounded_ref[:ROWS, :] = grad_q.astype(BF16)
        rounded_ref[ROWS:, :] = grad_p.astype(BF16)


def own_gradients(at, owner, row, hard, inner, came, sq, sp, gain, cq, tin, invp, q, p):
    full = lambda a: pl.BlockSpec(a.shape, lambda t: (0,) * a.ndim)
    size = DEEP * NX
    tall = pl.BlockSpec((size * ROWS, FEATURES), lambda t: (t, 0))
    whole = pl.BlockSpec((2 * ROWS, FEATURES), lambda t: (0, 0))
    return pl.pallas_call(
        own_kernel,
        grid=(NZ // DEEP,),
        in_specs=[pl.BlockSpec(memory_space=pltpu.SMEM)]
        + [full(a) for a in (owner, row, hard, inner)]
        + [pl.BlockSpec((size, 8, ROWS), lambda t: (t, 2, 0))]
        + [full(a) for a in (sq, sp, gain, cq, tin, invp)]
        + [tall]
        + piece_specs(),
        out_specs=[whole, whole],
        out_shape=[
            jax.ShapeDtypeStruct((2 * ROWS, FEATURES), F32),
            jax.ShapeDtypeStruct((2 * ROWS, FEATURES), BF16),
        ],
        scratch_shapes=[
            pltpu.VMEM((ROWS, FEATURES), F32),
            pltpu.VMEM((ROWS, FEATURES), F32),
            pltpu.VMEM((ROWS, ROWS), F32),
        ],
        compiler_params=pltpu.CompilerParams(vmem_limit_bytes=56 * 2**20),
        cost_estimate=pl.CostEstimate(
            flops=2 * 10**9, bytes_accessed=10 * 2**20, transcendentals=0
        ),
        name="own_gradients",
    )(at, owner, row, hard, inner, came, sq, sp, gain, cq, tin, invp, q, *p)


def final_kernel(
    x_ref, left_ref, near_ref, far_ref, gain_ref, q_ref, p0, p1, p2, p3, p4, out_ref
):
    step = pl.program_id(0)
    x = x_ref[0]

    @pl.when(step == 0)
    def _():
        out_ref[...] = jnp.zeros_like(out_ref)

    starts = [
        pl.multiple_of((i * NX + (x + NX - s) % NX) * ROWS, ROWS) for i in range(DEEP) for s in PLACES_X
    ]
    left = jnp.concatenate([left_ref[pl.ds(start, ROWS), :] for start in starts], axis=0)
    right = (near_ref[...].astype(F32) + far_ref[...].astype(F32)).astype(BF16)
    out_ref[...] += gain_ref[...] * (
        lax.dot_general(
            left, read_pieces((p0, p1, p2, p3, p4)), (((0,), (0,)), ((), ())),
            preferred_element_type=F32,
        )
        + jnp.dot(right, q_ref[...], preferred_element_type=F32)
    )


def final_product(at, left, near, far, gain, q, p):
    size = DEEP * NX * ROWS
    lanes = lambda n: pl.BlockSpec((n, size), lambda t: (0, t))
    tall = lambda n: pl.BlockSpec((size, n), lambda t: (t, 0))
    return pl.pallas_call(
        final_kernel,
        grid=(NZ // DEEP,),
        in_specs=[
            pl.BlockSpec(memory_space=pltpu.SMEM), tall(ROWS), lanes(ROWS), lanes(ROWS),
            pl.BlockSpec((1, FEATURES), lambda t: (0, 0)), tall(FEATURES),
        ]
        + piece_specs(),
        out_specs=pl.BlockSpec((ROWS, FEATURES), lambda t: (0, 0)),
        out_shape=jax.ShapeDtypeStruct((ROWS, FEATURES), F32),
        compiler_params=pltpu.CompilerParams(vmem_limit_bytes=56 * 2**20),
        cost_estimate=pl.CostEstimate(
            flops=2 * 10**9, bytes_accessed=12 * 2**20, transcendentals=0
        ),
        name="final_product",
    )(at, left, near, far, gain, q, *p)


STEPS_Y = (0, 1, 3, 2)


def body(attn, stream, out_proj, gain, neg_owner, neg_row):
    z, x = lax.axis_index("z"), lax.axis_index("x")
    y, core = lax.axis_index("y"), lax.axis_index("core")
    d, m = z * NX + x, y * NC + core

    blocks = out_proj.reshape(NY, NC, FEATURES, FEATURES)

    def by_core(c):
        kept = [
            lax.dynamic_slice(blocks, ((y - s) % NY, c, 0, 0), (1, 1, FEATURES, FEATURES))
            for s in STEPS_Y
        ]
        return jnp.concatenate(kept, axis=0).reshape(NY * FEATURES, FEATURES)

    proj_mine, proj_other = by_core(core), by_core(1 - core)

    block = attn.reshape(2 * ROWS, FEATURES)
    parts = [block] + [lax.ppermute(block, "y", shifted(NY, s)) for s in STEPS_Y[1:]]
    near = jnp.concatenate(parts, axis=1)
    far = lax.ppermute(near, "core", shifted(NC, 1))
    hidden = jnp.dot(near, proj_mine, preferred_element_type=F32)
    hidden = hidden + jnp.dot(far, proj_other, preferred_element_type=F32)
    scaled = (hidden + stream.reshape(2 * ROWS, FEATURES).astype(F32)) * gain[None, :]
    scaled_q, scaled_p = scaled[:ROWS], scaled[ROWS:]
    queries, passages = scaled_q.astype(BF16), scaled_p.astype(BF16)

    p_line = lax.all_gather(passages, "z", axis=0)
    p_pieces = pieces_x(p_line)

    column = gather_x(queries).reshape(NX * ROWS, FEATURES)
    q_all = lax.all_gather(column, "z", axis=0, tiled=True)

    def some_rows(kind):
        first = kind * ROWS + m * 16
        cut = [
            lax.dynamic_slice_in_dim(v, first, 16, 0).reshape(16, NY, FEATURES) for v in (near, far)
        ]
        both = jnp.stack([jnp.where(core == 0, cut[c], cut[1 - c]) for c in range(NC)])
        at = lambda a: jnp.where((y - a) % NY == 3, 2, jnp.where((y - a) % NY == 2, 3, (y - a) % NY))
        rows = [lax.dynamic_index_in_dim(both, at(a), 2, keepdims=False) for a in range(NY)]
        return jnp.stack(rows)

    mine = jnp.stack([some_rows(0), some_rows(1)])
    mine = mine.reshape(2, NZ, 16, NX, ROWS).transpose(1, 3, 0, 2, 4).reshape(N_DP, 32, ROWS)

    owner, row = neg_owner.T, neg_row.T
    order = jnp.arange(N_DP, dtype=jnp.int32)

    def dense(owners, values, empty):
        hit = owners[None] == order.reshape((N_DP,) + (1,) * owners.ndim)
        return jnp.sum(jnp.where(hit, values[None] - empty, 0), axis=1) + empty

    rows_own = dense(owner, row, -1)

    inner_part = lax.dot_general(
        passages, queries, (((1,), (1,)), ((), ())), preferred_element_type=F32
    )
    squares = jnp.stack([jnp.sum(scaled_q * scaled_q, axis=1), jnp.sum(scaled_p * scaled_p, axis=1)])
    part = jnp.concatenate([inner_part, squares, jnp.zeros((6, ROWS), F32)], axis=0)
    part, _ = lax.optimization_barrier((part, column))
    total = jnp.sum(lax.all_gather(part, MP, axis=0), axis=0)
    norm_q = jnp.sqrt(total[ROWS] + EPSILON)
    norm_p = jnp.sqrt(total[ROWS + 1] + EPSILON)
    inv_q, inv_p = 1.0 / norm_q, 1.0 / norm_p
    score = total[:ROWS] * inv_p[:, None] * inv_q[None, :]
    logit = score / WARMTH
    eye = jnp.eye(ROWS, dtype=bool)
    positive = jnp.sum(jnp.where(eye, logit, 0.0), axis=0)
    top = jnp.max(logit, axis=0)
    exps = jnp.exp(logit - top[None, :])
    exp_sum = jnp.sum(exps, axis=0)
    exps = (exps * inv_p[:, None] * inv_q[None, :]).astype(BF16)

    ids = (owner * ROWS + row)[m % NEG]
    high = lax.reduce_precision(inv_p, 8, 7)
    middle = lax.reduce_precision(inv_p - high, 8, 7)
    small = [(ids // ROWS), (ids % ROWS), high, middle, inv_p - high - middle]
    share = jnp.concatenate(
        [
            lax.dynamic_slice_in_dim(exps, m * 16, 16, 0),
            jnp.stack([v.astype(BF16) for v in small]),
            jnp.zeros((3, ROWS), BF16),
        ],
        axis=0,
    )
    share = jnp.concatenate([mine, jnp.broadcast_to(share[None], (N_DP, 24, ROWS))], axis=1)
    share, _ = lax.optimization_barrier((share, p_line))
    share = lax.all_to_all(share, DP, 0, 0, tiled=True)
    shares = lax.all_gather(share, MP, axis=0)

    row_iota = jnp.arange(ROWS, dtype=jnp.int32)
    named = rows_own[:, None, :] == row_iota[None, :, None]
    *close, share = lax.optimization_barrier(p_pieces[:3] + (share,))
    p_pieces = tuple(close) + p_pieces[3:]
    invp_all = jnp.sum(share[:, 50:53].astype(F32), axis=1)
    invp_named = jnp.sum(jnp.where(named, invp_all[:, :, None], 0.0), axis=1)
    raw_hard = jnp.zeros((NEG, ROWS), F32)
    for piece, s, first in zip(p_pieces, (0, 1, 3, 2, 2), (0, 0, 0, 0, NZ // 2)):
        here = (first + jnp.arange(piece.shape[0])) * NX + (x - s) % NX
        hit = owner[None] == here[:, None, None]
        row_here = jnp.sum(jnp.where(hit, row[None] + 1, 0), axis=1) - 1
        raw = lax.dot_general(
            piece.reshape(-1, FEATURES), queries, (((1,), (1,)), ((), ())), preferred_element_type=F32
        ).reshape(-1, ROWS, ROWS)
        raw = jnp.sum(jnp.where(row_here[:, None] == row_iota[None, :, None], raw, 0.0), axis=1)
        raw_hard = raw_hard + jnp.sum(jnp.where(hit, raw[:, None], 0.0), axis=0)

    def pick(values):
        hit = owner[:, None, :] == order[None, :, None]
        return jnp.sum(jnp.where(hit, values[None], 0.0), axis=1)

    invp_hard = pick(invp_named)
    copies = jnp.broadcast_to(raw_hard[None], (N_MP, NEG, ROWS))
    raw = jnp.sum(lax.all_to_all(copies, MP, 0, 0, tiled=True), axis=0)
    hard_score = raw * invp_hard * inv_q[None]
    hard_logit = hard_score / WARMTH
    peak = jnp.maximum(top, jnp.max(hard_logit, axis=0))
    log_total = peak + jnp.log(
        exp_sum * jnp.exp(top - peak) + jnp.sum(jnp.exp(hard_logit - peak[None]), axis=0)
    )
    query_loss = log_total - positive
    hard = GRAD_SCALE * jnp.exp(hard_logit - log_total[None]) * inv_q[None] * invp_hard
    hard = hard.astype(BF16).astype(F32)
    factor = GRAD_SCALE * jnp.exp(top - log_total)
    diag = GRAD_SCALE * (jnp.exp(positive - log_total) - 1.0) * inv_q * inv_p
    inner = jnp.where(eye, diag[None], exps.astype(F32) * factor[None])
    inner_rounded = inner.astype(BF16).astype(F32)
    weighted = inner_rounded * score * norm_p[:, None]
    is_own = owner == d
    cq = (jnp.sum(weighted, axis=0) + jnp.sum(hard * hard_score / invp_hard, axis=0)) * inv_q
    own_row = jnp.sum(jnp.where(is_own, row + 1, 0), axis=0) - 1
    own_hard = jnp.sum(jnp.where(is_own, hard * hard_score, 0.0), axis=0)
    inner_p = inner_rounded * score + jnp.where(row_iota[:, None] == own_row[None], own_hard[None], 0.0)
    tin = jnp.sum(inner_p * norm_q[None], axis=1) * inv_p
    carried = jnp.where(is_own, 0.0, hard_score * norm_q[None])

    def pieces(v):
        high = lax.reduce_precision(v, 8, 7)
        return [high, v - high]

    late = [hard] + pieces(carried) + [jnp.stack(pieces(factor) + [diag] + pieces(cq) + pieces(tin) + [diag])]
    late = jnp.concatenate([v.astype(BF16) for v in late], axis=0)
    late_half = lax.dynamic_slice_in_dim(late, core * (LATE // 2), LATE // 2, 0)
    sums = pieces(dense(owner, hard * carried, 0.0))
    named_there = [rows_own.astype(F32), dense(owner, hard, 0.0)] + sums
    named_there = jnp.stack([v.astype(BF16) for v in named_there] + [jnp.zeros((N_DP, ROWS), BF16)] * 4, axis=1)
    came = jnp.concatenate(
        [jnp.broadcast_to(late_half[None], (N_DP, LATE // 2, ROWS)), named_there], axis=1
    )
    came = lax.all_to_all(came, DP, 0, 0, tiled=True)
    late_half = came[:, : LATE // 2]
    late_other = lax.ppermute(late_half, "core", shifted(NC, 1))
    late_all = jnp.concatenate(
        [jnp.where(core == 0, late_half, late_other), jnp.where(core == 0, late_other, late_half)],
        axis=1,
    )

    line = lambda v: v.reshape(1, -1)
    grad_stream, rounded = own_gradients(
        jnp.stack([d, x]), owner, row, hard, inner, came, scaled_q, scaled_p,
        line(gain), line(cq), line(tin), line(inv_p), q_all, p_pieces,
    )

    back = lambda w: lax.dot_general(
        rounded, w, (((1,), (1,)), ((), ())), preferred_element_type=F32
    )
    came = lax.ppermute(back(proj_other).astype(BF16), "core", shifted(NC, 1))
    kept = back(proj_mine) + came.astype(F32)
    grad_attn = kept[:, :FEATURES]
    for i, s in list(enumerate(STEPS_Y))[1:]:
        block = kept[:, i * FEATURES : (i + 1) * FEATURES].astype(BF16)
        grad_attn = grad_attn + lax.ppermute(block, "y", shifted(NY, -s)).astype(F32)

    late_used, _ = lax.optimization_barrier((late_all, kept))
    left, right = coefficients(core, shares, late_used, invp_all)
    left_other = lax.ppermute(left, "core", shifted(NC, 1))
    right_other = lax.ppermute(right, "core", shifted(NC, 1))
    left = jnp.concatenate(
        [jnp.where(core == 0, left, left_other), jnp.where(core == 0, left_other, left)], axis=0
    )
    grad_weight = final_product(
        x.reshape(1), left, right, right_other, line(gain), q_all, p_pieces
    )
    return (
        query_loss,
        grad_stream.reshape(2, ROWS, FEATURES),
        grad_attn.reshape(2, ROWS, FEATURES),
        grad_weight,
    )


def solution(mesh):
    fine = Mesh(mesh.devices.reshape(NZ, NX, NY, NC), ("z", "x", "y", "core"))
    placed = (
        P(None, DP, MP),
        P(None, DP, MP),
        P(None, MP),
        P(MP),
        P(DP, None),
        P(DP, None),
    )
    return jax.shard_map(
        body,
        mesh=fine,
        in_specs=placed,
        out_specs=(P(DP), P(None, DP, MP), P(None, DP, MP), P(DP, MP)),
        check_vma=False,
    )
```

```python
import jax
import jax.numpy as jnp
from jax import lax
from jax.experimental import pallas as pl
from jax.experimental.pallas import tpu as pltpu
from jax.sharding import Mesh
from jax.sharding import PartitionSpec as P

WARMTH = 0.02
GRAD_SCALE = 16.0 / WARMTH
EPSILON = 1e-06
F32 = jnp.float32
BF16 = jnp.bfloat16
DP = ("z", "x")
MP = ("y", "core")
NZ, NX, NY, NC = 8, 4, 4, 2
N_DP, N_MP = NZ * NX, NY * NC
ROWS = 128
NEG = 8
ALL_ROWS = N_DP * ROWS
FEATURES = 512
WIDTH = N_MP * FEATURES
TILE = 1024
CHUNK = 4


def shifted(size, step):
    return [(i, (i + step) % size) for i in range(size)]


def place(buffer, block, index):
    return lax.dynamic_update_slice(buffer, block[None], (index,) + (0,) * block.ndim)


def gather_x(block):
    x = lax.axis_index("x")
    parts = [lax.ppermute(block, "x", shifted(NX, s)) for s in (1, 3, 2)]
    buffer = jnp.zeros((NX,) + block.shape, block.dtype)
    for s, part in zip((0, 1, 3, 2), [block] + parts):
        buffer = place(buffer, part, (x - s) % NX)
    return buffer


def pieces_x(line):
    left = lax.ppermute(line, "x", shifted(NX, 1))
    right = lax.ppermute(line, "x", shifted(NX, -1))
    low = lax.ppermute(left[: NZ // 2], "x", shifted(NX, 1))
    high = lax.ppermute(right[NZ // 2 :], "x", shifted(NX, -1))
    return line, left, right, low, high


PLACES_X = (0, 1, 3, 2)
DEEP = 2
LATE = 32


def late_rows(ref, j):
    r = ref[pl.ds(j, 1)].astype(F32)[0]
    return r[:8], r[8:16] + r[16:24], r[24:25] + r[25:26], r[26:27], r[27:28] + r[28:29], r[29:30] + r[30:31]


def index_rows(ref, j):
    r = ref[:, pl.ds(j, 1)].astype(F32)[:, 0]
    return r[:, 0].astype(jnp.int32), r[:, 1].astype(jnp.int32)


def shares_spec(groups, part, size=16):
    return pl.BlockSpec((N_MP, groups, size, ROWS), lambda t: (0, t, part, 0))


def piece_specs():
    block = (DEEP, ROWS, FEATURES)
    half = NZ // 2 // DEEP
    near = pl.BlockSpec(block, lambda t: (t, 0, 0))
    low = pl.BlockSpec(block, lambda t: (jnp.minimum(t, half - 1), 0, 0))
    high = pl.BlockSpec(block, lambda t: (jnp.maximum(t - half, 0), 0, 0))
    return [near, near, near, low, high]


def read_pieces(refs):
    line, left, right, low, high = refs
    is_low = pl.program_id(0) < NZ // 2 // DEEP
    rows = []
    for i in range(DEEP):
        rows += [line[i], left[i], right[i], jnp.where(is_low, low[i], high[i])]
    return jnp.concatenate(rows, axis=0)


def spread_dp(block):
    copies = jnp.broadcast_to(block[None], (N_DP,) + block.shape)
    return lax.all_to_all(copies, DP, 0, 0, tiled=True)


HALF = N_DP // 2


def coef_kernel(
    core_ref, index_ref, late_ref, exps_ref, aq_ref, ap_ref, invp_ref, whole_ref, left_ref, xp_ref,
    xq, apt_ref,
):
    step = pl.program_id(0)
    groups = TILE // ROWS
    core = core_ref[0]
    held = lambda o: ap_ref[:, pl.ds(core * HALF + o, 1)].reshape(ROWS, ROWS)

    @pl.when(step == 0)
    def _():
        xq[...] = jnp.zeros_like(xq)
        for o in range(HALF):
            apt_ref[:, o * ROWS : (o + 1) * ROWS] = held(o).astype(F32).T.astype(BF16)

    lates = [late_rows(late_ref, g) for g in range(groups)]
    indices = [index_rows(index_ref, g) for g in range(groups)]
    beside = lambda rows, i: jnp.concatenate([r[i] for r in rows], axis=1)
    hard_k, carried_k = beside(lates, 0), beside(lates, 1)
    owner, row = beside(indices, 0) - core * HALF, beside(indices, 1)
    aq = jnp.concatenate([aq_ref[:, g].reshape(ROWS, ROWS) for g in range(groups)], axis=0)
    order = lax.broadcasted_iota(jnp.int32, (HALF, TILE), 0)
    named = jnp.full((HALF, TILE), -1, jnp.int32)
    hard = jnp.zeros((HALF, TILE), F32)
    carried = jnp.zeros((HALF, TILE), F32)
    for k in range(NEG):
        hit = owner[k : k + 1] == order
        named = jnp.where(hit, row[k : k + 1], named)
        hard = jnp.where(hit, hard_k[k : k + 1], hard)
        carried = jnp.where(hit, carried_k[k : k + 1], carried)
    high = carried.astype(BF16)
    low = (carried - high.astype(F32)).astype(BF16)
    pad = jnp.zeros((ROWS - 2 * HALF, TILE), F32)
    extra = jnp.concatenate([high.astype(F32), low.astype(F32), pad], axis=0).T.astype(BF16)
    aq_ext = jnp.concatenate([aq, extra], axis=1)
    row_of = lax.broadcasted_iota(jnp.int32, (ROWS, TILE), 0)
    xp = jnp.zeros((ROWS, TILE), F32)
    for c in range(0, HALF, CHUNK):
        tiles = []
        for o in range(c, c + CHUNK):
            tile = jnp.where(row_of == named[o : o + 1], hard[o : o + 1], 0.0)
            tiles.append(tile.astype(BF16))
        coef = jnp.concatenate(tiles, axis=0)
        at = slice(c * ROWS, (c + CHUNK) * ROWS)
        xq[at, :] += jnp.dot(coef, aq_ext, preferred_element_type=F32)
        xp = xp + jnp.dot(apt_ref[:, at], coef, preferred_element_type=F32)
    xp_ref[...] = xp.astype(BF16)

    eye = lax.broadcasted_iota(jnp.int32, (ROWS, ROWS), 0) == lax.broadcasted_iota(
        jnp.int32, (ROWS, ROWS), 1
    )

    @pl.when(step // (HALF // groups) == core)
    def _():
        for part in range(groups):
            lanes = slice(part * ROWS, (part + 1) * ROWS)
            exps = exps_ref[:, part].reshape(ROWS, ROWS).astype(F32)
            inner = jnp.where(eye, lates[part][3], exps * lates[part][2]).astype(BF16)
            at = pl.ds(pl.multiple_of((step * groups + part - core * HALF) * ROWS, ROWS), ROWS)
            xq[at, :ROWS] += jnp.dot(inner, aq[lanes, :], preferred_element_type=F32)
            more = jnp.dot(apt_ref[:, at], inner, preferred_element_type=F32)
            more = more - aq[lanes, :].astype(F32).T * lates[part][4]
            xp_ref[:, lanes] = (xp_ref[:, lanes].astype(F32) + more).astype(BF16)

    @pl.when(step == pl.num_programs(0) - 1)
    def _():
        lane = lax.broadcasted_iota(jnp.int32, (ROWS, ROWS), 1)
        for o in range(HALF):
            at = slice(o * ROWS, (o + 1) * ROWS)
            sums = xq[at, ROWS:]
            mine = (lane == o) | (lane == HALF + o)
            hard_sum = jnp.sum(jnp.where(mine, sums, 0.0), axis=1, keepdims=True)
            across = lambda v: jnp.sum(jnp.where(eye, v, 0.0), axis=1, keepdims=True)
            all_o = core * HALF + o
            cp = hard_sum * across(invp_ref[pl.ds(all_o, 1), :]) + across(late_rows(whole_ref, all_o)[5])
            left_ref[at, :] = (xq[at, :ROWS] - held(o).astype(F32) * cp).astype(BF16)

def coefficients(core, shares, late, invp):
    full = lambda shape: pl.BlockSpec(shape, lambda t: (0,) * len(shape))
    held = HALF * ROWS
    groups = TILE // ROWS
    return pl.pallas_call(
        coef_kernel,
        grid=(ALL_ROWS // TILE,),
        in_specs=[
            pl.BlockSpec(memory_space=pltpu.SMEM), shares_spec(groups, 6, 8),
            pl.BlockSpec((groups, LATE, ROWS), lambda t: (t, 0, 0)),
            shares_spec(groups, 2), shares_spec(groups, 0),
            pl.BlockSpec((N_MP, N_DP, 16, ROWS), lambda t: (0, 0, 1, 0)), full((N_DP, ROWS)),
            full((N_DP, LATE, ROWS)),
        ],
        out_specs=[full((held, ROWS)), pl.BlockSpec((ROWS, TILE), lambda t: (0, t))],
        out_shape=[
            jax.ShapeDtypeStruct((held, ROWS), BF16),
            jax.ShapeDtypeStruct((ROWS, ALL_ROWS), BF16),
        ],
        scratch_shapes=[
            pltpu.VMEM((held, 2 * ROWS), F32),
            pltpu.VMEM((ROWS, held), BF16),
        ],
        compiler_params=pltpu.CompilerParams(vmem_limit_bytes=56 * 2**20),
        cost_estimate=pl.CostEstimate(
            flops=10 * 10**9, bytes_accessed=8 * 2**20, transcendentals=0
        ),
        name="coefficients",
    )(core.reshape(1), shares, late, shares, shares, shares, invp, late)

def own_kernel(
    d_ref, owner_ref, row_ref, hard_ref, inner_ref, came_ref, sq_ref, sp_ref,
    gain_ref, cq_ref, tin_ref, invp_ref, q_ref, p0, p1, p2, p3, p4, stream_ref, rounded_ref,
    acc_q, acc_p, acc_t,
):
    step = pl.program_id(0)
    d, x = d_ref[0], d_ref[1]

    @pl.when(step == 0)
    def _():
        acc_q[...] = jnp.zeros_like(acc_q)
        acc_p[...] = jnp.zeros_like(acc_p)
        acc_t[...] = jnp.zeros_like(acc_t)

    row_of = lax.broadcasted_iota(jnp.int32, (ROWS, ROWS), 0)
    down = lambda v: jnp.sum(v, axis=0, keepdims=True)
    tall, wide = [], []
    for g in range(DEEP * NX):
        plane, n = step * DEEP + g // NX, g % NX
        block = plane * NX + (x + NX - PLACES_X[n]) % NX
        inner = jnp.where(block == d, inner_ref[...], 0.0)
        hit = owner_ref[...] == block
        named = down(jnp.where(hit, row_ref[...] + 1, 0)) - 1
        hard = down(jnp.where(hit, hard_ref[...], 0.0))
        tall.append((jnp.where(row_of == named, hard, 0.0) + inner).astype(BF16))
        inner = jnp.where(plane * NX + n == d, inner_ref[...], 0.0)
        came = came_ref[g].astype(F32)
        named = row_of == came[0:1].astype(jnp.int32)
        hard, moved = came[1:2], came[2:3] + came[3:4]
        wide.append((jnp.where(named, hard, 0.0) + inner).astype(BF16))
        acc_t[...] += jnp.where(named, moved, 0.0)
    acc_q[...] += lax.dot_general(
        jnp.concatenate(tall, axis=0), read_pieces((p0, p1, p2, p3, p4)), (((0,), (0,)), ((), ())),
        preferred_element_type=F32,
    )
    acc_p[...] += jnp.dot(jnp.concatenate(wide, axis=1), q_ref[...], preferred_element_type=F32)

    @pl.when(step == pl.num_programs(0) - 1)
    def _():
        eye = row_of == lax.broadcasted_iota(jnp.int32, (ROWS, ROWS), 1)
        across = lambda ref: jnp.sum(jnp.where(eye, ref[...], 0.0), axis=1, keepdims=True)
        cp = across(tin_ref) + jnp.sum(acc_t[...], axis=1, keepdims=True) * across(invp_ref)
        grad_q = gain_ref[...] * (acc_q[...] - across(cq_ref) * sq_ref[...])
        grad_p = gain_ref[...] * (acc_p[...] - cp * sp_ref[...])
        stream_ref[:ROWS, :] = grad_q
        stream_ref[ROWS:, :] = grad_p
        rounded_ref[:ROWS, :] = grad_q.astype(BF16)
        rounded_ref[ROWS:, :] = grad_p.astype(BF16)


def own_gradients(at, owner, row, hard, inner, came, sq, sp, gain, cq, tin, invp, q, p):
    full = lambda a: pl.BlockSpec(a.shape, lambda t: (0,) * a.ndim)
    size = DEEP * NX
    tall = pl.BlockSpec((size * ROWS, FEATURES), lambda t: (t, 0))
    whole = pl.BlockSpec((2 * ROWS, FEATURES), lambda t: (0, 0))
    return pl.pallas_call(
        own_kernel,
        grid=(NZ // DEEP,),
        in_specs=[pl.BlockSpec(memory_space=pltpu.SMEM)]
        + [full(a) for a in (owner, row, hard, inner)]
        + [pl.BlockSpec((size, 8, ROWS), lambda t: (t, 2, 0))]
        + [full(a) for a in (sq, sp, gain, cq, tin, invp)]
        + [tall]
        + piece_specs(),
        out_specs=[whole, whole],
        out_shape=[
            jax.ShapeDtypeStruct((2 * ROWS, FEATURES), F32),
            jax.ShapeDtypeStruct((2 * ROWS, FEATURES), BF16),
        ],
        scratch_shapes=[
            pltpu.VMEM((ROWS, FEATURES), F32),
            pltpu.VMEM((ROWS, FEATURES), F32),
            pltpu.VMEM((ROWS, ROWS), F32),
        ],
        compiler_params=pltpu.CompilerParams(vmem_limit_bytes=56 * 2**20),
        cost_estimate=pl.CostEstimate(
            flops=2 * 10**9, bytes_accessed=10 * 2**20, transcendentals=0
        ),
        name="own_gradients",
    )(at, owner, row, hard, inner, came, sq, sp, gain, cq, tin, invp, q, *p)


def final_kernel(
    at_ref, mine_ref, other_ref, near_ref, far_ref, gain_ref, q_ref, p0, p1, p2, p3, p4, out_ref
):
    step = pl.program_id(0)
    x, core = at_ref[0], at_ref[1]

    @pl.when(step == 0)
    def _():
        out_ref[...] = jnp.zeros_like(out_ref)

    per_half = HALF // NX // DEEP
    is_mine = step // per_half == core
    left = []
    for i in range(DEEP):
        for s in PLACES_X:
            block = (step % per_half) * DEEP * NX + i * NX + (x + NX - s) % NX
            at = pl.ds(pl.multiple_of(block * ROWS, ROWS), ROWS)
            left.append(jnp.where(is_mine, mine_ref[at, :], other_ref[at, :]))
    left = jnp.concatenate(left, axis=0)
    right = (near_ref[...].astype(F32) + far_ref[...].astype(F32)).astype(BF16)
    out_ref[...] += gain_ref[...] * (
        lax.dot_general(
            left, read_pieces((p0, p1, p2, p3, p4)), (((0,), (0,)), ((), ())),
            preferred_element_type=F32,
        )
        + jnp.dot(right, q_ref[...], preferred_element_type=F32)
    )


def final_product(at, mine, other, near, far, gain, q, p):
    size = DEEP * NX * ROWS
    lanes = lambda n: pl.BlockSpec((n, size), lambda t: (0, t))
    tall = lambda n: pl.BlockSpec((size, n), lambda t: (t, 0))
    return pl.pallas_call(
        final_kernel,
        grid=(NZ // DEEP,),
        in_specs=[
            pl.BlockSpec(memory_space=pltpu.SMEM),
            pl.BlockSpec((HALF * ROWS, ROWS), lambda t: (0, 0)),
            pl.BlockSpec((HALF * ROWS, ROWS), lambda t: (0, 0)),
            lanes(ROWS), lanes(ROWS),
            pl.BlockSpec((1, FEATURES), lambda t: (0, 0)), tall(FEATURES),
        ]
        + piece_specs(),
        out_specs=pl.BlockSpec((ROWS, FEATURES), lambda t: (0, 0)),
        out_shape=jax.ShapeDtypeStruct((ROWS, FEATURES), F32),
        compiler_params=pltpu.CompilerParams(vmem_limit_bytes=56 * 2**20),
        cost_estimate=pl.CostEstimate(
            flops=2 * 10**9, bytes_accessed=12 * 2**20, transcendentals=0
        ),
        name="final_product",
    )(at, mine, other, near, far, gain, q, *p)


STEPS_Y = (0, 1, 3, 2)


def body(attn, stream, out_proj, gain, neg_owner, neg_row):
    z, x = lax.axis_index("z"), lax.axis_index("x")
    y, core = lax.axis_index("y"), lax.axis_index("core")
    d, m = z * NX + x, y * NC + core

    blocks = out_proj.reshape(NY, NC, FEATURES, FEATURES)

    def by_core(c):
        kept = [
            lax.dynamic_slice(blocks, ((y - s) % NY, c, 0, 0), (1, 1, FEATURES, FEATURES))
            for s in STEPS_Y
        ]
        return jnp.concatenate(kept, axis=0).reshape(NY * FEATURES, FEATURES)

    proj_mine, proj_other = by_core(core), by_core(1 - core)

    block = attn.reshape(2 * ROWS, FEATURES)
    parts = [block] + [lax.ppermute(block, "y", shifted(NY, s)) for s in STEPS_Y[1:]]
    near = jnp.concatenate(parts, axis=1)
    far = lax.ppermute(near, "core", shifted(NC, 1))
    hidden = jnp.dot(near, proj_mine, preferred_element_type=F32)
    hidden = hidden + jnp.dot(far, proj_other, preferred_element_type=F32)
    scaled = (hidden + stream.reshape(2 * ROWS, FEATURES).astype(F32)) * gain[None, :]
    scaled_q, scaled_p = scaled[:ROWS], scaled[ROWS:]
    queries, passages = scaled_q.astype(BF16), scaled_p.astype(BF16)

    p_line = lax.all_gather(passages, "z", axis=0)
    p_pieces = pieces_x(p_line)

    column = gather_x(queries).reshape(NX * ROWS, FEATURES)
    q_all = lax.all_gather(column, "z", axis=0, tiled=True)

    def some_rows(kind):
        first = kind * ROWS + m * 16
        cut = [
            lax.dynamic_slice_in_dim(v, first, 16, 0).reshape(16, NY, FEATURES) for v in (near, far)
        ]
        both = jnp.stack([jnp.where(core == 0, cut[c], cut[1 - c]) for c in range(NC)])
        at = lambda a: jnp.where((y - a) % NY == 3, 2, jnp.where((y - a) % NY == 2, 3, (y - a) % NY))
        rows = [lax.dynamic_index_in_dim(both, at(a), 2, keepdims=False) for a in range(NY)]
        return jnp.stack(rows)

    mine = jnp.stack([some_rows(0), some_rows(1)])
    mine = mine.reshape(2, NZ, 16, NX, ROWS).transpose(1, 3, 0, 2, 4).reshape(N_DP, 32, ROWS)

    owner, row = neg_owner.T, neg_row.T
    order = jnp.arange(N_DP, dtype=jnp.int32)

    def dense(owners, values, empty):
        hit = owners[None] == order.reshape((N_DP,) + (1,) * owners.ndim)
        return jnp.sum(jnp.where(hit, values[None] - empty, 0), axis=1) + empty

    rows_own = dense(owner, row, -1)

    inner_part = lax.dot_general(
        passages, queries, (((1,), (1,)), ((), ())), preferred_element_type=F32
    )
    squares = jnp.stack([jnp.sum(scaled_q * scaled_q, axis=1), jnp.sum(scaled_p * scaled_p, axis=1)])
    part = jnp.concatenate([inner_part, squares, jnp.zeros((6, ROWS), F32)], axis=0)
    part, _ = lax.optimization_barrier((part, column))
    total = jnp.sum(lax.all_gather(part, MP, axis=0), axis=0)
    norm_q = jnp.sqrt(total[ROWS] + EPSILON)
    norm_p = jnp.sqrt(total[ROWS + 1] + EPSILON)
    inv_q, inv_p = 1.0 / norm_q, 1.0 / norm_p
    score = total[:ROWS] * inv_p[:, None] * inv_q[None, :]
    logit = score / WARMTH
    eye = jnp.eye(ROWS, dtype=bool)
    positive = jnp.sum(jnp.where(eye, logit, 0.0), axis=0)
    top = jnp.max(logit, axis=0)
    exps = jnp.exp(logit - top[None, :])
    exp_sum = jnp.sum(exps, axis=0)
    exps = (exps * inv_p[:, None] * inv_q[None, :]).astype(BF16)

    ids = (owner * ROWS + row)[m % NEG]
    high = lax.reduce_precision(inv_p, 8, 7)
    middle = lax.reduce_precision(inv_p - high, 8, 7)
    small = [(ids // ROWS), (ids % ROWS), high, middle, inv_p - high - middle]
    share = jnp.concatenate(
        [
            lax.dynamic_slice_in_dim(exps, m * 16, 16, 0),
            jnp.stack([v.astype(BF16) for v in small]),
            jnp.zeros((3, ROWS), BF16),
        ],
        axis=0,
    )
    share = jnp.concatenate([mine, jnp.broadcast_to(share[None], (N_DP, 24, ROWS))], axis=1)
    share, _ = lax.optimization_barrier((share, p_line))
    share = lax.all_to_all(share, DP, 0, 0, tiled=True)
    shares = lax.all_gather(share, MP, axis=0)

    row_iota = jnp.arange(ROWS, dtype=jnp.int32)
    named = rows_own[:, None, :] == row_iota[None, :, None]
    close = lax.optimization_barrier(p_pieces[:3])
    *distant, share = lax.optimization_barrier(p_pieces[3:] + (share,))
    p_pieces = tuple(close) + tuple(distant)
    invp_all = jnp.sum(share[:, 50:53].astype(F32), axis=1)
    invp_named = jnp.sum(jnp.where(named, invp_all[:, :, None], 0.0), axis=1)
    raw_hard = jnp.zeros((NEG, ROWS), F32)
    for piece, s, first in zip(p_pieces, (0, 1, 3, 2, 2), (0, 0, 0, 0, NZ // 2)):
        here = (first + jnp.arange(piece.shape[0])) * NX + (x - s) % NX
        hit = owner[None] == here[:, None, None]
        row_here = jnp.sum(jnp.where(hit, row[None] + 1, 0), axis=1) - 1
        raw = lax.dot_general(
            piece.reshape(-1, FEATURES), queries, (((1,), (1,)), ((), ())), preferred_element_type=F32
        ).reshape(-1, ROWS, ROWS)
        raw = jnp.sum(jnp.where(row_here[:, None] == row_iota[None, :, None], raw, 0.0), axis=1)
        raw_hard = raw_hard + jnp.sum(jnp.where(hit, raw[:, None], 0.0), axis=0)

    def pick(values):
        hit = owner[:, None, :] == order[None, :, None]
        return jnp.sum(jnp.where(hit, values[None], 0.0), axis=1)

    invp_hard = pick(invp_named)
    copies = jnp.broadcast_to(raw_hard[None], (N_MP, NEG, ROWS))
    raw = jnp.sum(lax.all_to_all(copies, MP, 0, 0, tiled=True), axis=0)
    hard_score = raw * invp_hard * inv_q[None]
    hard_logit = hard_score / WARMTH
    peak = jnp.maximum(top, jnp.max(hard_logit, axis=0))
    log_total = peak + jnp.log(
        exp_sum * jnp.exp(top - peak) + jnp.sum(jnp.exp(hard_logit - peak[None]), axis=0)
    )
    query_loss = log_total - positive
    hard = GRAD_SCALE * jnp.exp(hard_logit - log_total[None]) * inv_q[None] * invp_hard
    hard = hard.astype(BF16).astype(F32)
    factor = GRAD_SCALE * jnp.exp(top - log_total)
    diag = GRAD_SCALE * (jnp.exp(positive - log_total) - 1.0) * inv_q * inv_p
    inner = jnp.where(eye, diag[None], exps.astype(F32) * factor[None])
    inner_rounded = inner.astype(BF16).astype(F32)
    weighted = inner_rounded * score * norm_p[:, None]
    is_own = owner == d
    cq = (jnp.sum(weighted, axis=0) + jnp.sum(hard * hard_score / invp_hard, axis=0)) * inv_q
    own_row = jnp.sum(jnp.where(is_own, row + 1, 0), axis=0) - 1
    own_hard = jnp.sum(jnp.where(is_own, hard * hard_score, 0.0), axis=0)
    inner_p = inner_rounded * score + jnp.where(row_iota[:, None] == own_row[None], own_hard[None], 0.0)
    tin = jnp.sum(inner_p * norm_q[None], axis=1) * inv_p
    carried = jnp.where(is_own, 0.0, hard_score * norm_q[None])

    def pieces(v):
        high = lax.reduce_precision(v, 8, 7)
        return [high, v - high]

    late = [hard] + pieces(carried) + [jnp.stack(pieces(factor) + [diag] + pieces(cq) + pieces(tin) + [diag])]
    late = jnp.concatenate([v.astype(BF16) for v in late], axis=0)
    late_half = lax.dynamic_slice_in_dim(late, core * (LATE // 2), LATE // 2, 0)
    sums = pieces(dense(owner, hard * carried, 0.0))
    named_there = [rows_own.astype(F32), dense(owner, hard, 0.0)] + sums
    named_there = jnp.stack([v.astype(BF16) for v in named_there] + [jnp.zeros((N_DP, ROWS), BF16)] * 4, axis=1)
    came = jnp.concatenate(
        [jnp.broadcast_to(late_half[None], (N_DP, LATE // 2, ROWS)), named_there], axis=1
    )
    came = lax.all_to_all(came, DP, 0, 0, tiled=True)
    late_half = came[:, : LATE // 2]
    late_other = lax.ppermute(late_half, "core", shifted(NC, 1))
    late_all = jnp.concatenate(
        [jnp.where(core == 0, late_half, late_other), jnp.where(core == 0, late_other, late_half)],
        axis=1,
    )

    line = lambda v: v.reshape(1, -1)
    grad_stream, rounded = own_gradients(
        jnp.stack([d, x]), owner, row, hard, inner, came, scaled_q, scaled_p,
        line(gain), line(cq), line(tin), line(inv_p), q_all, p_pieces,
    )

    back = lambda w: lax.dot_general(
        rounded, w, (((1,), (1,)), ((), ())), preferred_element_type=F32
    )
    came = lax.ppermute(back(proj_other).astype(BF16), "core", shifted(NC, 1))
    kept = lax.optimization_barrier(back(proj_mine)) + came.astype(F32)
    received = []
    for i, s in list(enumerate(STEPS_Y))[1:]:
        block = kept[:, i * FEATURES : (i + 1) * FEATURES].astype(BF16)
        received.append(lax.ppermute(block, "y", shifted(NY, -s)))

    late_used, _ = lax.optimization_barrier((late_all, kept))
    left, right = coefficients(core, shares, late_used, invp_all)
    left, right, *received = lax.optimization_barrier((left, right, *received))
    grad_attn = kept[:, :FEATURES] + sum(v.astype(F32) for v in received)
    left_other = lax.ppermute(left, "core", shifted(NC, 1))
    right_other = lax.ppermute(right, "core", shifted(NC, 1))
    grad_weight = final_product(
        jnp.stack([x, core]), left, left_other, right, right_other, line(gain), q_all, p_pieces
    )
    return (
        query_loss,
        grad_stream.reshape(2, ROWS, FEATURES),
        grad_attn.reshape(2, ROWS, FEATURES),
        grad_weight,
    )


def solution(mesh):
    fine = Mesh(mesh.devices.reshape(NZ, NX, NY, NC), ("z", "x", "y", "core"))
    placed = (
        P(None, DP, MP),
        P(None, DP, MP),
        P(None, MP),
        P(MP),
        P(DP, None),
        P(DP, None),
    )
    return jax.shard_map(
        body,
        mesh=fine,
        in_specs=placed,
        out_specs=(P(DP), P(None, DP, MP), P(None, DP, MP), P(DP, MP)),
        check_vma=False,
    )
```
